32 devices in a mesh: ctx: 8 (over z, x), rep: 4 (over y, core).
Axes of the slice: x: 2, y: 2, z: 4, core: 2. Of those that a mesh axis runs over, the one named last changes fastest.
Arguments:
- queries: bfloat16 [8, 2, 128, 192], P('rep', None, 'ctx'), parts along dimension 0, may hold values from -6 to 6
- key_absorb: bfloat16 [128, 128, 512], P('ctx'), may hold values from -0.5 to 0.5
- latent_cache: bfloat16 [8, 32768, 576], P('rep', 'ctx'), parts along dimension 0, may hold values from -600 to 600
- page_order: int32 [8, 256], P('rep', 'ctx'), parts along dimension 0, may hold values from 0 to 255, each once within a row
- lengths: int32 [8], P('rep'), parts along dimension 0, may hold values from 8192 to 32768
- kerple_scale: float32 [128], replicated, may hold values from 0.05 to 2
- kerple_rate: float32 [128], replicated, may hold values from 0.005 to 0.5
- value_up: bfloat16 [128, 512, 128], P('ctx'), may hold values from -0.25 to 0.25
- output_weight: bfloat16 [16384, 7168], P('ctx'), may hold values from -0.0625 to 0.0625
Outputs:
- attn_out: bfloat16 [8, 2, 7168], P('rep', None, 'ctx'), parts along dimension 0
The draws below stay inside these ranges and needn't reach their ends.
There are 4 independent parts, one for each index of `rep`. The reference program is written for one: setup_inputs(seed, part) draws one part's arguments, and reference() takes and returns one part's arrays. A program takes and returns all parts, laid end to end along the dimension named above; an argument that names none is the same for every part. Nothing has to cross between parts.
All inputs are finite; a program needn't handle non-finite values.
Results may differ from the reference program's by a relative error of at most 0.015.
Values may be sent and summed in bfloat16 or wider, within the bound.
No kernel may reach another device: no remote copies, remote signals or barrier semaphores. Data moves between devices by JAX's collectives and lax.ppermute only.
A program may use at most 192 MiB of HBM per device.

```python
import math
import jax
import jax.numpy as jnp
from jax import lax

HEADS = 128
NOPE = 128
ROPE = 64
LAT = 512
VDIM = 128
D = 7168
REQ = 2
QLEN = 2
PAGE = 128
CTXLEN = 32768
PAGES = 256


def draw_latent_cache(key, part):
    key = jax.random.fold_in(key, 7)
    base_key = jax.random.fold_in(key, 0)
    full_shape = (REQ, CTXLEN, LAT + ROPE)
    baseline = jnp.clip(jax.random.normal(base_key, full_shape, jnp.float32), -6.0, 6.0)
    values = baseline
    return values.astype(jnp.bfloat16)


def strengthened(array, own_key, source, target, blocks, factor):
    owner, partner = [(jnp.arange(array.shape[position]) // (array.shape[position] // blocks)).reshape([-1 if axis == position else 1 for axis in range(array.ndim)]) for position in (source, target)]
    chosen = jax.random.permutation(own_key, blocks)[partner]
    strong = (owner == chosen) | (owner == (partner + blocks // 2) % blocks)
    return jnp.where(strong, factor * array, array)


def steps_of(own_key, shape, shards, low, top_value):
    factor_of = 1.0
    for dim, blocks in shards:
        draws = jax.random.uniform(jax.random.fold_in(jax.random.fold_in(own_key, 6), dim), (blocks,), jnp.float32, low / len(shards), top_value / len(shards))
        factor_of = factor_of * jnp.repeat(jnp.exp(draws), shape[dim] // blocks).reshape((-1,) + (1,) * (len(shape) - 1 - dim))
    return factor_of


def noise(own_key, dims, scale, limit, cuts=(), held_as=jnp.bfloat16):
    values = scale * jax.random.normal(own_key, dims, jnp.float32)
    if cuts:
        values = values * steps_of(own_key, dims, cuts, -0.22, 0.18)
    return jnp.clip(values, -limit, limit).astype(held_as)


def noise_with(rng, dims, width, bound, pieces, heavy, held_as=jnp.bfloat16):
    result = width * jax.random.normal(rng, dims, jnp.float32)
    if pieces:
        result = result * steps_of(rng, dims, pieces, -0.22, 0.18)
    return jnp.clip(strengthened(result, jax.random.fold_in(rng, 3), *heavy), -bound, bound).astype(held_as)


def setup_inputs(seed: int = 0, part: int = 0) -> dict:
    seeds = jax.random.split(jax.random.key(seed), 10)
    part_keys = jax.random.split(jax.random.fold_in(seeds[9], part), 10)
    return {
        "queries": noise(part_keys[0], (REQ, QLEN, HEADS, NOPE + ROPE), 1.0, 6.0, ((2, 8),)),
        "key_absorb": noise(seeds[1], (HEADS, NOPE, LAT), NOPE ** -0.5, 0.5, ((0, 8),)),
        "latent_cache": draw_latent_cache(jax.random.fold_in(jax.random.fold_in(seeds[9], part), 71), part),
        "page_order": jax.vmap(lambda own: jax.random.permutation(own, PAGES))(jax.random.split(part_keys[3], REQ)).reshape((REQ, PAGES)).astype(jnp.int32),
        "lengths": jax.random.randint(part_keys[4], (REQ,), CTXLEN // 4, CTXLEN + 1).astype(jnp.int32),
        "kerple_scale": jnp.clip(jnp.exp(jax.random.uniform(seeds[5], (HEADS,), jnp.float32, math.log(0.05), math.log(2.0))), 0.05, 2.0),
        "kerple_rate": jnp.clip(jnp.exp(jax.random.uniform(seeds[6], (HEADS,), jnp.float32, math.log(0.005), math.log(0.5))), 0.005, 0.5),
        "value_up": noise(seeds[7], (HEADS, LAT, VDIM), LAT ** -0.5, 0.25, ((0, 8),)),
        "output_weight": noise_with(seeds[8], (HEADS * VDIM, D), (HEADS * VDIM) ** -0.5, 0.0625, ((0, 8),), (0, 1, 8, 2.0)),
    }


masked_score = -1.0e30


def reference(queries, key_absorb, latent_cache, page_order, lengths, kerple_scale, kerple_rate, value_up, output_weight):
    latent_query = jnp.einsum('bqhn,hnc->bqhc', queries[..., :NOPE].astype(jnp.float32), key_absorb.astype(jnp.float32)).astype(jnp.bfloat16)
    full_query = jnp.concatenate([latent_query, queries[..., NOPE:]], axis=-1)
    offsets = jnp.arange(PAGE, dtype=jnp.int32)
    key_pos = (page_order[:, :, None] * PAGE + offsets[None, None, :]).reshape(REQ, CTXLEN).astype(jnp.int32)
    query_pos = (lengths[:, None] - QLEN + jnp.arange(QLEN, dtype=jnp.int32)[None, :]).astype(jnp.int32)
    softmax_scale = (NOPE + ROPE) ** -0.5

    def per_request(items):
        request_query, request_cache, request_keys, request_pos = items
        distance = request_pos[:, None] - request_keys[None, :]
        visible = distance >= 0
        spread = jnp.maximum(distance, 0).astype(jnp.float32)
        flat_query = request_query.reshape(QLEN * HEADS, LAT + ROPE)
        scores = jnp.dot(flat_query, request_cache.T, preferred_element_type=jnp.float32).reshape(QLEN, HEADS, CTXLEN)
        log_bias = kerple_scale[None, :, None] * jnp.log1p(kerple_rate[None, :, None] * spread[:, None, :])
        scores = jnp.where(visible[:, None, :], scores * softmax_scale - log_bias, masked_score)
        row_max = jnp.max(scores, axis=-1, keepdims=True)
        weights = jnp.where(visible[:, None, :], jnp.exp(scores - row_max), 0.0)
        row_total = jnp.sum(weights, axis=-1)
        summed = jnp.dot(weights.reshape(QLEN * HEADS, CTXLEN).astype(jnp.bfloat16), request_cache[:, :LAT], preferred_element_type=jnp.float32)
        return (summed.reshape(QLEN, HEADS, LAT) / row_total[..., None]).astype(jnp.bfloat16)

    attn_latent = lax.map(per_request, (full_query, latent_cache, key_pos, query_pos))
    up_values = jnp.einsum('bqhc,hcv->bqhv', attn_latent.astype(jnp.float32), value_up.astype(jnp.float32)).astype(jnp.bfloat16)
    flat_values = up_values.reshape(REQ * QLEN, HEADS * VDIM)
    return jnp.dot(flat_values, output_weight, preferred_element_type=jnp.float32).reshape(REQ, QLEN, D).astype(jnp.bfloat16)
```

```python
import functools

import jax
import jax.numpy as jnp
from jax import lax
from jax.experimental import pallas as pl
from jax.experimental.pallas import tpu as pltpu
from jax.sharding import PartitionSpec as P

NOPE = 128
ROPE = 64
LAT = 512
PAGE = 128
LANES = 128
LAT_TILES = LAT // LANES
LOG2E = 1.4426950408889634
SOFTMAX_SCALE = (NOPE + ROPE) ** (-0.5)
LOWEST = -1e30
STAT_ROWS = 16


def head_of_row(shape, heads):
    return lax.rem(lax.broadcasted_iota(jnp.int32, shape, 0), heads)


def query_kernel(queries_hbm, absorb_hbm, out_ref, again_ref, queries_ref, absorb_ref, sems):
    rows = queries_ref.shape[0]
    heads = absorb_ref.shape[0]
    half = rows // 2
    pieces = sems.shape[0] - 1
    group = heads // pieces
    copies = [pltpu.make_async_copy(queries_hbm, queries_ref, sems.at[pieces])] + [
        pltpu.make_async_copy(
            absorb_hbm.at[pl.ds(i * group, group)],
            absorb_ref.at[pl.ds(i * group, group)],
            sems.at[i],
        )
        for i in range(pieces)
    ]
    for copy in copies:
        copy.start()
    copies[0].wait()
    nope = queries_ref[:, :NOPE]
    owner = head_of_row((rows, NOPE), heads)
    latent = jnp.zeros((rows, LAT), jnp.float32)
    for i in range(pieces):
        spread = jnp.concatenate(
            [
                jnp.where(owner == h, nope, jnp.zeros_like(nope))
                for h in range(i * group, (i + 1) * group)
            ],
            axis=1,
        )
        copies[i + 1].wait()
        latent += jnp.dot(
            spread,
            absorb_ref[i * group : (i + 1) * group].reshape(group * NOPE, LAT),
            preferred_element_type=jnp.float32,
        )
    latent = latent.astype(jnp.bfloat16)
    rope = queries_ref[:, NOPE:]
    rope = jnp.concatenate([rope[:half], rope[half:]], axis=1)
    for b in range(2):
        for j in range(LAT_TILES):
            start = (b * LAT_TILES + j) * half
            out_ref[start : start + half, :] = latent[
                b * half : (b + 1) * half, j * LANES : (j + 1) * LANES
            ]
    out_ref[2 * LAT_TILES * half :, :] = rope
    again_ref[...] = out_ref[...]


def column_kernel(rate_ref, scale_ref, through_ref, inv_rate_ref, scales_ref, passed_ref):
    del through_ref, passed_ref
    ctx, heads, _ = inv_rate_ref.shape
    line = ctx // 2
    me = lax.axis_index("ctx")
    for source, target in ((1.0 / rate_ref[...], inv_rate_ref), (scale_ref[...], scales_ref)):
        size = source.shape[1]
        same = lax.broadcasted_iota(jnp.int32, (size, size), 0) == lax.broadcasted_iota(
            jnp.int32, (size, size), 1
        )
        column = jnp.sum(jnp.where(same, source, 0.0), axis=1, keepdims=True)
        column = jnp.broadcast_to(column, (size, LANES)).reshape(ctx, heads, LANES)
        for k in range(ctx):
            owner = me ^ (2 * (k % line) + k // line)
            picked = jnp.zeros((heads, LANES), jnp.float32)
            for device in range(ctx):
                picked = jnp.where(owner == device, column[device], picked)
            target[k] = picked


def attention_kernel(pages_ref, lengths_ref, *refs, ctx, b):
    query_refs, refs = refs[:ctx], refs[ctx:]
    cache_ref, inv_rate, scale, near_ref, far_ref, query, acc, total, *buffers = refs
    scores_of, weights_of, factor_of = buffers[:2], buffers[2:4], buffers[4:]
    rows, chunk = scores_of[0].shape
    half = rows // ctx
    heads = half // 2
    line = ctx // 2
    steps = cache_ref.shape[2] // chunk
    pair_width = 2 * PAGE
    pairs = chunk // pair_width
    request_rows = LAT_TILES * half
    start = b * request_rows

    for k, block in enumerate(query_refs):
        own = slice(k * half, (k + 1) * half)
        for j in range(LAT_TILES):
            query[own, j * LANES : (j + 1) * LANES] = block[
                start + j * half : start + (j + 1) * half, :
            ]
        query[own, LAT:] = block[2 * request_rows :, b * ROPE : (b + 1) * ROPE]

    lane = lax.broadcasted_iota(jnp.int32, (heads, LANES), 1)
    first_pos = lengths_ref[b] - 2

    def raw_scores(at):
        return jnp.dot(
            query[...],
            cache_ref[b, :, at * pair_width : (at + 1) * pair_width],
            preferred_element_type=jnp.float32,
        )

    def add_products(step):
        weights, factor = weights_of[step % 2], factor_of[step % 2]
        for columns in (slice(0, LAT // 2), slice(LAT // 2, LAT)):
            new = lax.dot_general(
                weights[...],
                cache_ref[b, columns, step * chunk : (step + 1) * chunk],
                (((1,), (1,)), ((), ())),
                preferred_element_type=jnp.float32,
            )
            for j in range(columns.start, columns.stop, LANES):
                part = new[:, j - columns.start : j - columns.start + LANES]
                at = slice(j, j + LANES)
                acc[:, at] = acc[:, at] * factor[...] + part if step else part

    top = jnp.full((rows, LANES), LOWEST, jnp.float32)
    ahead = raw_scores(0)
    for step in range(steps):
        scores, weights = scores_of[step % 2], weights_of[step % 2]
        tops = [None, None]
        for pair in range(pairs):
            raw = ahead
            at = step * pairs + pair
            if at + 1 < steps * pairs:
                ahead = raw_scores(at + 1)
            for side in range(2):
                page = pair * 2 + side
                columns = slice(page * PAGE, (page + 1) * PAGE)
                part = raw[:, side * PAGE : (side + 1) * PAGE].reshape(ctx, 2, heads, PAGE)
                base = first_pos - pages_ref[b, step * (chunk // PAGE) + page] * PAGE
                values = []
                for q in range(2):
                    distance = base + q - lane
                    spread = jnp.where(distance >= 0, distance.astype(jnp.float32), jnp.inf)
                    logs = jnp.log2(spread[None] + inv_rate[...])
                    value = part[:, q] * (SOFTMAX_SCALE * LOG2E) - scale[...] * logs
                    tops[q] = value if tops[q] is None else jnp.maximum(tops[q], value)
                    values.append(value)
                scores[:, columns] = jnp.stack(values, axis=1).reshape(rows, PAGE)
        lane_top = jnp.stack(tops, axis=1).reshape(rows, LANES)
        before = top
        top = jnp.maximum(before, jnp.max(lane_top, axis=1, keepdims=True))
        factor = jnp.exp2(before - top)
        factor_of[step % 2][...] = factor
        if step:
            add_products(step - 1)
        lane_total = total[...] * factor if step else jnp.zeros((rows, LANES), jnp.float32)
        for page in range(chunk // PAGE):
            columns = slice(page * PAGE, (page + 1) * PAGE)
            value = jnp.exp2(scores[:, columns] - top)
            lane_total += value
            weights[:, columns] = value.astype(jnp.bfloat16)
        total[...] = lane_total
    add_products(steps - 1)

    row_total = jnp.sum(total[...], axis=1, keepdims=True)
    row_total = jnp.broadcast_to(row_total, (rows, LANES))
    seen = row_total > 0.0
    safe = jnp.where(seen, row_total, 1.0)
    share = 1.0 / safe
    for j in range(LAT_TILES):
        columns = slice(j * LANES, (j + 1) * LANES)
        part = (acc[:, columns] * share).astype(jnp.bfloat16).reshape(ctx, half, LANES)
        near_ref[:, j * half : (j + 1) * half, :] = part[:line]
        far_ref[:, j * half : (j + 1) * half, :] = part[line:]
    log_total = jnp.where(seen, top + jnp.log2(safe), LOWEST).reshape(ctx, half, LANES)
    across = jnp.sum(jnp.where(diagonal(half), log_total, 0.0), axis=1, keepdims=True)
    packed = three_parts(across).astype(jnp.bfloat16)
    near_ref[:, request_rows:, :] = packed[:line]
    far_ref[:, request_rows:, :] = packed[line:]


def diagonal(half):
    return lax.broadcasted_iota(jnp.int32, (half, LANES), 0) == lax.broadcasted_iota(
        jnp.int32, (half, LANES), 1
    )


def three_parts(value):
    high = value.astype(jnp.bfloat16).astype(jnp.float32)
    middle = (value - high).astype(jnp.bfloat16).astype(jnp.float32)
    low = value - high - middle
    row = lax.broadcasted_iota(jnp.int32, (value.shape[0], STAT_ROWS, LANES), 1)
    return jnp.where(
        row == 0, high, jnp.where(row == 1, middle, jnp.where(row == 2, low, 0.0))
    )


def logs_of(stats):
    return jnp.sum(stats.astype(jnp.float32), axis=1, keepdims=True)


def as_column(across, half):
    return jnp.sum(jnp.where(diagonal(half), across, 0.0), axis=-1, keepdims=True)


def merge_kernel(own_ref, other_ref, *out_refs):
    request_rows = own_ref.shape[1] - STAT_ROWS
    half = request_rows // LAT_TILES
    own_log = logs_of(own_ref[:, request_rows:, :])
    other_log = logs_of(other_ref[:, request_rows:, :])
    high = jnp.maximum(own_log, other_log)
    own_factor = jnp.exp2(own_log - high)
    other_factor = jnp.exp2(other_log - high)
    both = own_factor + other_factor
    stats = three_parts(high + jnp.log2(both)).astype(jnp.bfloat16)
    own_factor = as_column(own_factor / both, half)
    other_factor = as_column(other_factor / both, half)
    for j in range(LAT_TILES):
        at = slice(j * half, (j + 1) * half)
        merged = (
            own_ref[:, at, :].astype(jnp.float32) * own_factor
            + other_ref[:, at, :].astype(jnp.float32) * other_factor
        ).astype(jnp.bfloat16)
        for k, out_ref in enumerate(out_refs):
            out_ref[at, :] = merged[k]
    for k, out_ref in enumerate(out_refs):
        out_ref[request_rows:, :] = stats[k]


def output_kernel(*refs):
    *part_refs, up_ref, weight_ref, out_ref, values, attn = refs
    heads = up_ref.shape[0]
    half = 2 * heads
    rows = 2 * half
    request_rows = LAT_TILES * half
    for b in range(2):
        parts = part_refs[b * len(part_refs) // 2 : (b + 1) * len(part_refs) // 2]
        logs = logs_of(jnp.stack([part[request_rows:, :] for part in parts]))
        factor = jnp.exp2(logs - jnp.max(logs, axis=0, keepdims=True))
        factor = as_column(factor / jnp.sum(factor, axis=0, keepdims=True), half)
        for j in range(LAT_TILES):
            at = slice(j * half, (j + 1) * half)
            attn[b * half : (b + 1) * half, j * LANES : (j + 1) * LANES] = sum(
                part[at, :].astype(jnp.float32) * factor[k] for k, part in enumerate(parts)
            ).astype(jnp.bfloat16)
    latent = attn[...]
    owner = head_of_row(latent.shape, heads)
    up = jnp.zeros((rows, up_ref.shape[2]), jnp.float32)
    for h in range(heads):
        own = jnp.where(owner == h, latent, jnp.zeros_like(latent))
        up += jnp.dot(own, up_ref[h], preferred_element_type=jnp.float32)
    up = up.astype(jnp.bfloat16)
    owner = head_of_row(up.shape, heads)
    spread = jnp.concatenate(
        [jnp.where(owner == h, up, jnp.zeros_like(up)) for h in range(heads)], axis=1
    )
    token = lax.broadcasted_iota(jnp.int32, (8, rows), 0)
    group = lax.broadcasted_iota(jnp.int32, (8, rows), 1) // heads
    pick = jnp.where(token == group, 1.0, 0.0).astype(jnp.bfloat16)
    values[...] = jnp.dot(pick, spread, preferred_element_type=jnp.float32)
    project(values, weight_ref, out_ref, True)


def project(values, weight_ref, out_ref, far):
    blocks, tokens, width = out_ref.shape
    bit = lax.rem(lax.axis_index("ctx") // 2, 2)
    first = (1 - bit if far else bit) * (2 * width)

    @pl.loop(0, blocks // 2)
    def _(k):
        result = jnp.dot(
            values[...].astype(jnp.bfloat16),
            weight_ref[:, pl.ds(pl.multiple_of(first + k * (4 * width), LANES), 2 * width)],
            preferred_element_type=jnp.float32,
        )
        out_ref[2 * k] = result[:tokens, :width].astype(out_ref.dtype)
        out_ref[2 * k + 1] = result[:tokens, width:].astype(out_ref.dtype)


def near_kernel(values, weight_ref, out_ref):
    project(values, weight_ref, out_ref, False)


def add_kernel(own_ref, other_ref, kept_ref, *sent_refs):
    me = lax.axis_index("ctx")
    own = (me // 4) * 2 + lax.rem(me, 2)
    for k, out_ref in enumerate((kept_ref,) + sent_refs):
        block = own_ref[own ^ k] + other_ref[own ^ k].astype(jnp.float32)
        out_ref[...] = block.astype(out_ref.dtype)


def sum_kernel(own_ref, *refs):
    *other_refs, out_ref = refs
    result = own_ref[...]
    for other in other_refs:
        result += other[...].astype(jnp.float32)
    requests, tokens, _ = out_ref.shape
    for b in range(requests):
        out_ref[b] = result[b * tokens : (b + 1) * tokens].astype(out_ref.dtype)


def per_device(
    queries,
    key_absorb,
    latent_cache,
    page_order,
    lengths,
    kerple_scale,
    kerple_rate,
    value_up,
    output_weight,
    *,
    ctx,
):
    requests, query_len, heads, query_width = queries.shape
    keys_dev = latent_cache.shape[1]
    half = query_len * heads
    rows = requests * half
    request_rows = LAT_TILES * half
    width = output_weight.shape[1] // ctx
    chunk = 1024

    hint = pl.CostEstimate(flops=20 * 10**9, bytes_accessed=2**20, transcendentals=0)
    long_hint = pl.CostEstimate(flops=100 * 10**9, bytes_accessed=2**20, transcendentals=0)
    in_hbm = lambda value: pltpu.with_memory_space_constraint(value, pltpu.HBM)
    in_vmem = lambda value: pltpu.with_memory_space_constraint(value, pltpu.VMEM)
    line = ctx // 2
    swap = lambda value, bits: lax.ppermute(value, "ctx", [(i, i ^ bits) for i in range(ctx)])
    packed, again = pl.pallas_call(
        query_kernel,
        in_specs=[pl.BlockSpec(memory_space=pl.ANY)] * 2,
        out_shape=[jax.ShapeDtypeStruct((2 * request_rows + half, LANES), jnp.bfloat16)] * 2,
        scratch_shapes=[
            pltpu.VMEM((rows, query_width), jnp.bfloat16),
            pltpu.VMEM(key_absorb.shape, jnp.bfloat16),
            pltpu.SemaphoreType.DMA((5,)),
        ],
        compiler_params=pltpu.CompilerParams(vmem_limit_bytes=8 * 2**20),
        name="latent_query",
    )(in_hbm(queries.reshape(rows, query_width)), in_hbm(key_absorb))
    columns = (ctx, heads, LANES)
    inv_rate, scale, again = pl.pallas_call(
        column_kernel,
        in_specs=[pl.BlockSpec(memory_space=pltpu.VMEM)] * 2
        + [pl.BlockSpec(memory_space=pl.ANY)],
        out_specs=[pl.BlockSpec(memory_space=pltpu.VMEM)] * 2
        + [pl.BlockSpec(memory_space=pl.ANY)],
        out_shape=[jax.ShapeDtypeStruct(columns, jnp.float32)] * 2
        + [jax.ShapeDtypeStruct(again.shape, again.dtype)],
        input_output_aliases={2: 2},
        compiler_params=pltpu.CompilerParams(vmem_limit_bytes=4 * 2**20),
        name="head_columns",
        cost_estimate=long_hint,
    )(in_hbm(kerple_rate.reshape(1, -1)), in_hbm(kerple_scale.reshape(1, -1)), again)
    column = [packed] + [swap(packed, 2 * k) for k in range(1, line)]
    gathered = column + [swap(value, 1) for value in [again] + column[1:]]

    cache = in_vmem(jnp.swapaxes(latent_cache, 1, 2))
    all_rows = ctx * half
    message = (request_rows + STAT_ROWS, LANES)
    in_smem = pl.BlockSpec(memory_space=pltpu.SMEM)
    whole = pl.BlockSpec(memory_space=pltpu.VMEM)
    parts = []
    for b in range(requests):
        near, far = pl.pallas_call(
            functools.partial(attention_kernel, ctx=ctx, b=b),
            in_specs=[in_smem, in_smem] + [whole] * (ctx + 3),
            out_shape=[jax.ShapeDtypeStruct((line,) + message, jnp.bfloat16)] * 2,
            scratch_shapes=[
                pltpu.VMEM((all_rows, LAT + ROPE), jnp.bfloat16),
                pltpu.VMEM((all_rows, LAT), jnp.float32),
                pltpu.VMEM((all_rows, LANES), jnp.float32),
            ]
            + [pltpu.VMEM((all_rows, chunk), jnp.float32)] * 2
            + [pltpu.VMEM((all_rows, chunk), jnp.bfloat16)] * 2
            + [pltpu.VMEM((all_rows, LANES), jnp.float32)] * 2,
            compiler_params=pltpu.CompilerParams(vmem_limit_bytes=8 * 2**20),
            cost_estimate=hint,
            name="attention",
        )(in_hbm(page_order), in_hbm(lengths), *gathered, cache, inv_rate, scale)
        merged = pl.pallas_call(
            merge_kernel,
            out_shape=[jax.ShapeDtypeStruct(message, jnp.bfloat16) for _ in range(line)],
            compiler_params=pltpu.CompilerParams(vmem_limit_bytes=4 * 2**20),
            name="merge",
        )(near, swap(far, 1))
        parts.append(merged[0])
        parts += [swap(merged[k], 2 * k) for k in range(1, line)]

    tokens = requests * query_len
    weight = in_vmem(output_weight)
    small = pltpu.CompilerParams(vmem_limit_bytes=4 * 2**20)
    far, values = pl.pallas_call(
        output_kernel,
        out_shape=[
            jax.ShapeDtypeStruct((line, tokens, width), jnp.bfloat16),
            jax.ShapeDtypeStruct((8, output_weight.shape[0]), jnp.float32),
        ],
        scratch_shapes=[pltpu.VMEM((rows, LAT), jnp.bfloat16)],
        compiler_params=small,
        cost_estimate=hint,
        name="up_and_far_output",
    )(*parts, in_vmem(value_up), weight)
    near = pl.pallas_call(
        near_kernel,
        out_shape=jax.ShapeDtypeStruct((line, tokens, width), jnp.float32),
        compiler_params=small,
        cost_estimate=hint,
        name="near_output",
    )(values, weight)
    block = (tokens, width)
    kept, *sent = pl.pallas_call(
        add_kernel,
        out_shape=[jax.ShapeDtypeStruct(block, jnp.float32)]
        + [jax.ShapeDtypeStruct(block, jnp.bfloat16)] * 3,
        compiler_params=small,
        name="add_columns",
    )(near, swap(far, 2))
    return pl.pallas_call(
        sum_kernel,
        out_shape=jax.ShapeDtypeStruct((requests, query_len, width), jnp.bfloat16),
        compiler_params=small,
        name="sum_output",
    )(kept, *(swap(part, bits) for part, bits in zip(sent, (1, 4, 5))))


def plain_device(
    queries,
    key_absorb,
    latent_cache,
    page_order,
    lengths,
    kerple_scale,
    kerple_rate,
    value_up,
    output_weight,
    *,
    ctx,
):
    requests, query_len, heads, _ = queries.shape
    width = output_weight.shape[1] // ctx
    latent_query = jnp.einsum(
        "bqhn,hnc->bqhc", queries[..., :NOPE], key_absorb, preferred_element_type=jnp.float32
    ).astype(jnp.bfloat16)
    own_query = jnp.concatenate([latent_query, queries[..., NOPE:]], axis=-1)
    full_query = lax.all_gather(own_query, "ctx", axis=2, tiled=True)
    offsets = jnp.arange(PAGE, dtype=jnp.int32)
    key_pos = (page_order[:, :, None] * PAGE + offsets).reshape(requests, -1)
    query_pos = lengths[:, None] - query_len + jnp.arange(query_len, dtype=jnp.int32)
    distance = query_pos[:, :, None] - key_pos[:, None, :]
    visible = (distance >= 0)[:, :, None, :]
    spread = jnp.maximum(distance, 0).astype(jnp.float32)[:, :, None, :]
    log_bias = kerple_scale[:, None] * jnp.log(1.0 + kerple_rate[:, None] * spread)
    scores = jnp.einsum(
        "bqhc,btc->bqht", full_query, latent_cache, preferred_element_type=jnp.float32
    )
    scores = jnp.where(visible, scores * SOFTMAX_SCALE - log_bias, LOWEST)
    row_max = jnp.max(scores, axis=-1)
    weights = jnp.where(visible, jnp.exp(scores - row_max[..., None]), 0.0)
    summed = jnp.einsum(
        "bqht,btc->bqhc",
        weights.astype(jnp.bfloat16),
        latent_cache[..., :LAT],
        preferred_element_type=jnp.float32,
    )
    factor = jnp.exp(row_max - lax.pmax(row_max, "ctx"))
    shared_total = lax.psum_scatter(
        jnp.sum(weights, axis=-1) * factor, "ctx", scatter_dimension=2, tiled=True
    )
    shared_sum = lax.psum_scatter(
        summed * factor[..., None], "ctx", scatter_dimension=2, tiled=True
    )
    attn_latent = (shared_sum / shared_total[..., None]).astype(jnp.bfloat16)
    up_values = jnp.einsum(
        "bqhc,hcv->bqhv", attn_latent, value_up, preferred_element_type=jnp.float32
    ).astype(jnp.bfloat16)
    partial_out = jnp.dot(
        up_values.reshape(requests * query_len, -1),
        output_weight,
        preferred_element_type=jnp.float32,
    )
    summed_out = lax.psum_scatter(partial_out, "ctx", scatter_dimension=1, tiled=True)
    return summed_out.astype(jnp.bfloat16).reshape(requests, query_len, width)


def solution(mesh):
    ctx = mesh.shape["ctx"]
    in_specs = (
        P("rep", None, "ctx", None),
        P("ctx", None, None),
        P("rep", "ctx", None),
        P("rep", "ctx"),
        P("rep"),
        P(),
        P(),
        P("ctx", None, None),
        P("ctx", None),
    )
    out_specs = P("rep", None, "ctx")

    def device_program(*args):
        heads = args[0].shape[2]
        width = args[-1].shape[1] // ctx
        tiled = ctx == 8 and heads % 16 == 0 and width % LANES == 0
        return (per_device if tiled else plain_device)(*args, ctx=ctx)

    return jax.shard_map(
        device_program, mesh=mesh, in_specs=in_specs, out_specs=out_specs, check_vma=False
    )
```

```python
import functools

import jax
import jax.numpy as jnp
from jax import lax
from jax.experimental import pallas as pl
from jax.experimental.pallas import tpu as pltpu
from jax.sharding import PartitionSpec as P

NOPE = 128
ROPE = 64
LAT = 512
PAGE = 128
LANES = 128
LAT_TILES = LAT // LANES
LOG2E = 1.4426950408889634
SOFTMAX_SCALE = (NOPE + ROPE) ** (-0.5)
LOWEST = -1e30
STAT_ROWS = 16


def head_of_row(shape, heads):
    return lax.rem(lax.broadcasted_iota(jnp.int32, shape, 0), heads)


def query_kernel(queries_hbm, absorb_hbm, out_ref, again_ref, queries_ref, absorb_ref, sems):
    rows = queries_ref.shape[0]
    heads = absorb_ref.shape[0]
    half = rows // 2
    pieces = sems.shape[0] - 1
    group = heads // pieces
    copies = [pltpu.make_async_copy(queries_hbm, queries_ref, sems.at[pieces])] + [
        pltpu.make_async_copy(
            absorb_hbm.at[pl.ds(i * group, group)],
            absorb_ref.at[pl.ds(i * group, group)],
            sems.at[i],
        )
        for i in range(pieces)
    ]
    for copy in copies:
        copy.start()
    copies[0].wait()
    nope = queries_ref[:, :NOPE]
    owner = head_of_row((rows, NOPE), heads)
    latent = jnp.zeros((rows, LAT), jnp.float32)
    for i in range(pieces):
        spread = jnp.concatenate(
            [
                jnp.where(owner == h, nope, jnp.zeros_like(nope))
                for h in range(i * group, (i + 1) * group)
            ],
            axis=1,
        )
        copies[i + 1].wait()
        latent += jnp.dot(
            spread,
            absorb_ref[i * group : (i + 1) * group].reshape(group * NOPE, LAT),
            preferred_element_type=jnp.float32,
        )
    latent = latent.astype(jnp.bfloat16)
    rope = queries_ref[:, NOPE:]
    rope = jnp.concatenate([rope[:half], rope[half:]], axis=1)
    for b in range(2):
        for j in range(LAT_TILES):
            start = (b * LAT_TILES + j) * half
            out_ref[start : start + half, :] = latent[
                b * half : (b + 1) * half, j * LANES : (j + 1) * LANES
            ]
    out_ref[2 * LAT_TILES * half :, :] = rope
    again_ref[...] = out_ref[...]


def lanes_kernel(rate_ref, scale_ref, through_ref, inv_rate_ref, scales_ref, passed_ref, *, ctx):
    del through_ref, passed_ref
    line = ctx // 2
    me = lax.axis_index("ctx")
    for source, target in ((1.0 / rate_ref[...], inv_rate_ref), (scale_ref[...], scales_ref)):
        size = source.shape[1]
        heads = size // ctx
        same = lax.broadcasted_iota(jnp.int32, (size, size), 0) == lax.broadcasted_iota(
            jnp.int32, (size, size), 1
        )
        column = jnp.sum(jnp.where(same, source, 0.0), axis=1, keepdims=True)
        column = jnp.broadcast_to(column, (size, LANES)).reshape(ctx, heads, LANES)
        rows = []
        for k in range(ctx):
            owner = me ^ (2 * (k % line) + k // line)
            picked = jnp.zeros((heads, LANES), jnp.float32)
            for device in range(ctx):
                picked = jnp.where(owner == device, column[device], picked)
            rows += [picked, picked]
        rows = jnp.concatenate(rows, axis=0)
        for i in range(rows.shape[0] // LANES):
            at = slice(i * LANES, (i + 1) * LANES)
            target[:, at] = rows[at].T[: target.shape[0]]


def attention_kernel(pages_ref, lengths_ref, *refs, ctx, b):
    query_refs, refs = refs[:ctx], refs[ctx:]
    cache_ref, inv_rate, scale, near_ref, far_ref, query, acc, *buffers = refs
    scores_of, weights_of, factor_of = buffers[:2], buffers[2:4], buffers[4:]
    chunk, rows = scores_of[0].shape
    half = rows // ctx
    heads = half // 2
    line = ctx // 2
    steps = cache_ref.shape[2] // chunk
    pair_width = 2 * PAGE
    pairs = chunk // pair_width
    request_rows = LAT_TILES * half
    start = b * request_rows

    for k, block in enumerate(query_refs):
        own = slice(k * half, (k + 1) * half)
        for j in range(LAT_TILES):
            query[own, j * LANES : (j + 1) * LANES] = block[
                start + j * half : start + (j + 1) * half, :
            ]
        query[own, LAT:] = block[2 * request_rows :, b * ROPE : (b + 1) * ROPE]

    first_pos = lengths_ref[b] - 2
    token = lax.rem(lax.broadcasted_iota(jnp.int32, (1, rows), 1) // heads, 2)
    own_rate, own_scale = inv_rate[0:1, :], scale[0:1, :]
    slot = lax.broadcasted_iota(jnp.int32, (PAGE, rows), 0)

    def raw_scores(at):
        return lax.dot_general(
            cache_ref[b, :, at * pair_width : (at + 1) * pair_width],
            query[...],
            (((0,), (1,)), ((), ())),
            preferred_element_type=jnp.float32,
        )

    def add_products(step):
        weights, factor = weights_of[step % 2], factor_of[step % 2]
        for at in (slice(0, LAT // 2), slice(LAT // 2, LAT)):
            new = jnp.dot(
                cache_ref[b, at, step * chunk : (step + 1) * chunk],
                weights[...],
                preferred_element_type=jnp.float32,
            )
            acc[at, :] = acc[at, :] * factor[0:1, :] + new if step else new

    top = jnp.full((1, rows), LOWEST, jnp.float32)
    total = jnp.zeros((1, rows), jnp.float32)
    ahead = raw_scores(0)
    for step in range(steps):
        scores, weights = scores_of[step % 2], weights_of[step % 2]
        tops = jnp.full((8, rows), LOWEST, jnp.float32)
        for pair in range(pairs):
            raw = ahead
            at = step * pairs + pair
            if at + 1 < steps * pairs:
                ahead = raw_scores(at + 1)
            for side in range(2):
                page = pair * 2 + side
                base = first_pos - pages_ref[b, step * (chunk // PAGE) + page] * PAGE
                distance = (base + token) - slot
                spread = jnp.where(distance >= 0, distance.astype(jnp.float32), jnp.inf)
                logs = jnp.log2(spread + own_rate)
                value = (
                    raw[side * PAGE : (side + 1) * PAGE] * (SOFTMAX_SCALE * LOG2E)
                    - own_scale * logs
                )
                tops = jnp.maximum(tops, jnp.max(value.reshape(PAGE // 8, 8, rows), axis=0))
                scores[page * PAGE : (page + 1) * PAGE, :] = value
        before = top
        top = jnp.maximum(before, jnp.max(tops, axis=0, keepdims=True))
        factor = jnp.exp2(before - top)
        factor_of[step % 2][...] = jnp.broadcast_to(factor, (8, rows))
        if step:
            add_products(step - 1)
        sums = jnp.zeros((8, rows), jnp.float32)
        for page in range(chunk // PAGE):
            at = slice(page * PAGE, (page + 1) * PAGE)
            value = jnp.exp2(scores[at, :] - top)
            sums += jnp.sum(value.reshape(PAGE // 8, 8, rows), axis=0)
            weights[at, :] = value.astype(jnp.bfloat16)
        total = total * factor + jnp.sum(sums, axis=0, keepdims=True)
    add_products(steps - 1)

    seen = total > 0.0
    safe = jnp.where(seen, total, 1.0)
    share = 1.0 / safe
    logs = jnp.where(seen, top + jnp.log2(safe), LOWEST)
    logs = jnp.broadcast_to(logs, (LANES, rows))
    turned = []
    for i in range(rows // LANES):
        at = slice(i * LANES, (i + 1) * LANES)
        turned.append(logs[:, at].T)
        first, count = i * LANES // half, LANES // half
        for j in range(LAT_TILES):
            part = (acc[j * LANES : (j + 1) * LANES, at] * share[:, at]).T
            part = part.astype(jnp.bfloat16).reshape(count, half, LANES)
            for k in range(count):
                to_ref, block = (near_ref, first + k) if first + k < line else (
                    far_ref,
                    first + k - line,
                )
                to_ref[block, j * half : (j + 1) * half, :] = part[k]
    log_total = jnp.concatenate(turned, axis=0).reshape(ctx, half, LANES)
    across = jnp.sum(jnp.where(diagonal(half), log_total, 0.0), axis=1, keepdims=True)
    packed = three_parts(across).astype(jnp.bfloat16)
    near_ref[:, request_rows:, :] = packed[:line]
    far_ref[:, request_rows:, :] = packed[line:]


def diagonal(half):
    return lax.broadcasted_iota(jnp.int32, (half, LANES), 0) == lax.broadcasted_iota(
        jnp.int32, (half, LANES), 1
    )


def three_parts(value):
    high = value.astype(jnp.bfloat16).astype(jnp.float32)
    middle = (value - high).astype(jnp.bfloat16).astype(jnp.float32)
    low = value - high - middle
    row = lax.broadcasted_iota(jnp.int32, (value.shape[0], STAT_ROWS, LANES), 1)
    return jnp.where(
        row == 0, high, jnp.where(row == 1, middle, jnp.where(row == 2, low, 0.0))
    )


def logs_of(stats):
    return jnp.sum(stats.astype(jnp.float32), axis=1, keepdims=True)


def as_column(across, half):
    return jnp.sum(jnp.where(diagonal(half), across, 0.0), axis=-1, keepdims=True)


def merge_kernel(own_ref, other_ref, *out_refs):
    request_rows = own_ref.shape[1] - STAT_ROWS
    half = request_rows // LAT_TILES
    own_log = logs_of(own_ref[:, request_rows:, :])
    other_log = logs_of(other_ref[:, request_rows:, :])
    high = jnp.maximum(own_log, other_log)
    own_factor = jnp.exp2(own_log - high)
    other_factor = jnp.exp2(other_log - high)
    both = own_factor + other_factor
    stats = three_parts(high + jnp.log2(both)).astype(jnp.bfloat16)
    own_factor = as_column(own_factor / both, half)
    other_factor = as_column(other_factor / both, half)
    for j in range(LAT_TILES):
        at = slice(j * half, (j + 1) * half)
        merged = (
            own_ref[:, at, :].astype(jnp.float32) * own_factor
            + other_ref[:, at, :].astype(jnp.float32) * other_factor
        ).astype(jnp.bfloat16)
        for k, out_ref in enumerate(out_refs):
            out_ref[at, :] = merged[k]
    for k, out_ref in enumerate(out_refs):
        out_ref[request_rows:, :] = stats[k]


def output_kernel(*refs):
    *part_refs, up_ref, weight_ref, out_ref, values, attn = refs
    heads = up_ref.shape[0]
    half = 2 * heads
    rows = 2 * half
    request_rows = LAT_TILES * half
    for b in range(2):
        parts = part_refs[b * len(part_refs) // 2 : (b + 1) * len(part_refs) // 2]
        logs = logs_of(jnp.stack([part[request_rows:, :] for part in parts]))
        factor = jnp.exp2(logs - jnp.max(logs, axis=0, keepdims=True))
        factor = as_column(factor / jnp.sum(factor, axis=0, keepdims=True), half)
        for j in range(LAT_TILES):
            at = slice(j * half, (j + 1) * half)
            attn[b * half : (b + 1) * half, j * LANES : (j + 1) * LANES] = sum(
                part[at, :].astype(jnp.float32) * factor[k] for k, part in enumerate(parts)
            ).astype(jnp.bfloat16)
    latent = attn[...]
    owner = head_of_row(latent.shape, heads)
    up = jnp.zeros((rows, up_ref.shape[2]), jnp.float32)
    for h in range(heads):
        own = jnp.where(owner == h, latent, jnp.zeros_like(latent))
        up += jnp.dot(own, up_ref[h], preferred_element_type=jnp.float32)
    up = up.astype(jnp.bfloat16)
    owner = head_of_row(up.shape, heads)
    spread = jnp.concatenate(
        [jnp.where(owner == h, up, jnp.zeros_like(up)) for h in range(heads)], axis=1
    )
    token = lax.broadcasted_iota(jnp.int32, (8, rows), 0)
    group = lax.broadcasted_iota(jnp.int32, (8, rows), 1) // heads
    pick = jnp.where(token == group, 1.0, 0.0).astype(jnp.bfloat16)
    values[...] = jnp.dot(pick, spread, preferred_element_type=jnp.float32)
    project(values, weight_ref, out_ref, True)


def project(values, weight_ref, out_ref, far):
    blocks, tokens, width = out_ref.shape
    bit = lax.rem(lax.axis_index("ctx") // 2, 2)
    first = (1 - bit if far else bit) * (2 * width)

    @pl.loop(0, blocks // 2)
    def _(k):
        result = jnp.dot(
            values[...].astype(jnp.bfloat16),
            weight_ref[:, pl.ds(pl.multiple_of(first + k * (4 * width), LANES), 2 * width)],
            preferred_element_type=jnp.float32,
        )
        out_ref[2 * k] = result[:tokens, :width].astype(out_ref.dtype)
        out_ref[2 * k + 1] = result[:tokens, width:].astype(out_ref.dtype)


def near_kernel(values, weight_ref, out_ref):
    project(values, weight_ref, out_ref, False)


def add_kernel(own_ref, other_ref, kept_ref, *sent_refs):
    me = lax.axis_index("ctx")
    own = (me // 4) * 2 + lax.rem(me, 2)
    for k, out_ref in enumerate((kept_ref,) + sent_refs):
        block = own_ref[own ^ k] + other_ref[own ^ k].astype(jnp.float32)
        out_ref[...] = block.astype(out_ref.dtype)


def sum_kernel(own_ref, *refs):
    *other_refs, out_ref = refs
    result = own_ref[...]
    for other in other_refs:
        result += other[...].astype(jnp.float32)
    requests, tokens, _ = out_ref.shape
    for b in range(requests):
        out_ref[b] = result[b * tokens : (b + 1) * tokens].astype(out_ref.dtype)


def per_device(
    queries,
    key_absorb,
    latent_cache,
    page_order,
    lengths,
    kerple_scale,
    kerple_rate,
    value_up,
    output_weight,
    *,
    ctx,
):
    requests, query_len, heads, query_width = queries.shape
    keys_dev = latent_cache.shape[1]
    half = query_len * heads
    rows = requests * half
    request_rows = LAT_TILES * half
    width = output_weight.shape[1] // ctx
    chunk = 1024

    hint = pl.CostEstimate(flops=20 * 10**9, bytes_accessed=2**20, transcendentals=0)
    long_hint = pl.CostEstimate(flops=100 * 10**9, bytes_accessed=2**20, transcendentals=0)
    in_hbm = lambda value: pltpu.with_memory_space_constraint(value, pltpu.HBM)
    in_vmem = lambda value: pltpu.with_memory_space_constraint(value, pltpu.VMEM)
    line = ctx // 2
    swap = lambda value, bits: lax.ppermute(value, "ctx", [(i, i ^ bits) for i in range(ctx)])
    packed, again = pl.pallas_call(
        query_kernel,
        in_specs=[pl.BlockSpec(memory_space=pl.ANY)] * 2,
        out_shape=[jax.ShapeDtypeStruct((2 * request_rows + half, LANES), jnp.bfloat16)] * 2,
        scratch_shapes=[
            pltpu.VMEM((rows, query_width), jnp.bfloat16),
            pltpu.VMEM(key_absorb.shape, jnp.bfloat16),
            pltpu.SemaphoreType.DMA((5,)),
        ],
        compiler_params=pltpu.CompilerParams(vmem_limit_bytes=8 * 2**20),
        name="latent_query",
    )(in_hbm(queries.reshape(rows, query_width)), in_hbm(key_absorb))
    by_row = (8, ctx * half)
    inv_rate, scale, again = pl.pallas_call(
        functools.partial(lanes_kernel, ctx=ctx),
        in_specs=[pl.BlockSpec(memory_space=pltpu.VMEM)] * 2
        + [pl.BlockSpec(memory_space=pl.ANY)],
        out_specs=[pl.BlockSpec(memory_space=pltpu.VMEM)] * 2
        + [pl.BlockSpec(memory_space=pl.ANY)],
        out_shape=[jax.ShapeDtypeStruct(by_row, jnp.float32)] * 2
        + [jax.ShapeDtypeStruct(again.shape, again.dtype)],
        input_output_aliases={2: 2},
        compiler_params=pltpu.CompilerParams(vmem_limit_bytes=4 * 2**20),
        name="head_lanes",
        cost_estimate=long_hint,
    )(in_hbm(kerple_rate.reshape(1, -1)), in_hbm(kerple_scale.reshape(1, -1)), again)
    column = [packed] + [swap(packed, 2 * k) for k in range(1, line)]
    gathered = column + [swap(value, 1) for value in [again] + column[1:]]

    cache = in_vmem(jnp.swapaxes(latent_cache, 1, 2))
    all_rows = ctx * half
    message = (request_rows + STAT_ROWS, LANES)
    in_smem = pl.BlockSpec(memory_space=pltpu.SMEM)
    whole = pl.BlockSpec(memory_space=pltpu.VMEM)
    parts = []
    for b in range(requests):
        near, far = pl.pallas_call(
            functools.partial(attention_kernel, ctx=ctx, b=b),
            in_specs=[in_smem, in_smem] + [whole] * (ctx + 3),
            out_shape=[jax.ShapeDtypeStruct((line,) + message, jnp.bfloat16)] * 2,
            scratch_shapes=[
                pltpu.VMEM((all_rows, LAT + ROPE), jnp.bfloat16),
                pltpu.VMEM((LAT, all_rows), jnp.float32),
            ]
            + [pltpu.VMEM((chunk, all_rows), jnp.float32)] * 2
            + [pltpu.VMEM((chunk, all_rows), jnp.bfloat16)] * 2
            + [pltpu.VMEM((8, all_rows), jnp.float32)] * 2,
            compiler_params=pltpu.CompilerParams(vmem_limit_bytes=8 * 2**20),
            cost_estimate=hint,
            name="attention",
        )(in_hbm(page_order), in_hbm(lengths), *gathered, cache, inv_rate, scale)
        merged = pl.pallas_call(
            merge_kernel,
            out_shape=[jax.ShapeDtypeStruct(message, jnp.bfloat16) for _ in range(line)],
            compiler_params=pltpu.CompilerParams(vmem_limit_bytes=4 * 2**20),
            name="merge",
        )(near, swap(far, 1))
        parts.append(merged[0])
        parts += [swap(merged[k], 2 * k) for k in range(1, line)]

    tokens = requests * query_len
    weight = in_vmem(output_weight)
    small = pltpu.CompilerParams(vmem_limit_bytes=4 * 2**20)
    far, values = pl.pallas_call(
        output_kernel,
        out_shape=[
            jax.ShapeDtypeStruct((line, tokens, width), jnp.bfloat16),
            jax.ShapeDtypeStruct((8, output_weight.shape[0]), jnp.float32),
        ],
        scratch_shapes=[pltpu.VMEM((rows, LAT), jnp.bfloat16)],
        compiler_params=small,
        cost_estimate=hint,
        name="up_and_far_output",
    )(*parts, in_vmem(value_up), weight)
    near = pl.pallas_call(
        near_kernel,
        out_shape=jax.ShapeDtypeStruct((line, tokens, width), jnp.float32),
        compiler_params=small,
        cost_estimate=hint,
        name="near_output",
    )(values, weight)
    block = (tokens, width)
    kept, *sent = pl.pallas_call(
        add_kernel,
        out_shape=[jax.ShapeDtypeStruct(block, jnp.float32)]
        + [jax.ShapeDtypeStruct(block, jnp.bfloat16)] * 3,
        compiler_params=small,
        name="add_columns",
    )(near, swap(far, 2))
    return pl.pallas_call(
        sum_kernel,
        out_shape=jax.ShapeDtypeStruct((requests, query_len, width), jnp.bfloat16),
        compiler_params=small,
        name="sum_output",
    )(kept, *(swap(part, bits) for part, bits in zip(sent, (1, 4, 5))))


def plain_device(
    queries,
    key_absorb,
    latent_cache,
    page_order,
    lengths,
    kerple_scale,
    kerple_rate,
    value_up,
    output_weight,
    *,
    ctx,
):
    requests, query_len, heads, _ = queries.shape
    width = output_weight.shape[1] // ctx
    latent_query = jnp.einsum(
        "bqhn,hnc->bqhc", queries[..., :NOPE], key_absorb, preferred_element_type=jnp.float32
    ).astype(jnp.bfloat16)
    own_query = jnp.concatenate([latent_query, queries[..., NOPE:]], axis=-1)
    full_query = lax.all_gather(own_query, "ctx", axis=2, tiled=True)
    offsets = jnp.arange(PAGE, dtype=jnp.int32)
    key_pos = (page_order[:, :, None] * PAGE + offsets).reshape(requests, -1)
    query_pos = lengths[:, None] - query_len + jnp.arange(query_len, dtype=jnp.int32)
    distance = query_pos[:, :, None] - key_pos[:, None, :]
    visible = (distance >= 0)[:, :, None, :]
    spread = jnp.maximum(distance, 0).astype(jnp.float32)[:, :, None, :]
    log_bias = kerple_scale[:, None] * jnp.log(1.0 + kerple_rate[:, None] * spread)
    scores = jnp.einsum(
        "bqhc,btc->bqht", full_query, latent_cache, preferred_element_type=jnp.float32
    )
    scores = jnp.where(visible, scores * SOFTMAX_SCALE - log_bias, LOWEST)
    row_max = jnp.max(scores, axis=-1)
    weights = jnp.where(visible, jnp.exp(scores - row_max[..., None]), 0.0)
    summed = jnp.einsum(
        "bqht,btc->bqhc",
        weights.astype(jnp.bfloat16),
        latent_cache[..., :LAT],
        preferred_element_type=jnp.float32,
    )
    factor = jnp.exp(row_max - lax.pmax(row_max, "ctx"))
    shared_total = lax.psum_scatter(
        jnp.sum(weights, axis=-1) * factor, "ctx", scatter_dimension=2, tiled=True
    )
    shared_sum = lax.psum_scatter(
        summed * factor[..., None], "ctx", scatter_dimension=2, tiled=True
    )
    attn_latent = (shared_sum / shared_total[..., None]).astype(jnp.bfloat16)
    up_values = jnp.einsum(
        "bqhc,hcv->bqhv", attn_latent, value_up, preferred_element_type=jnp.float32
    ).astype(jnp.bfloat16)
    partial_out = jnp.dot(
        up_values.reshape(requests * query_len, -1),
        output_weight,
        preferred_element_type=jnp.float32,
    )
    summed_out = lax.psum_scatter(partial_out, "ctx", scatter_dimension=1, tiled=True)
    return summed_out.astype(jnp.bfloat16).reshape(requests, query_len, width)


def solution(mesh):
    ctx = mesh.shape["ctx"]
    in_specs = (
        P("rep", None, "ctx", None),
        P("ctx", None, None),
        P("rep", "ctx", None),
        P("rep", "ctx"),
        P("rep"),
        P(),
        P(),
        P("ctx", None, None),
        P("ctx", None),
    )
    out_specs = P("rep", None, "ctx")

    def device_program(*args):
        heads = args[0].shape[2]
        width = args[-1].shape[1] // ctx
        tiled = ctx == 8 and heads % 16 == 0 and width % LANES == 0
        return (per_device if tiled else plain_device)(*args, ctx=ctx)

    return jax.shard_map(
        device_program, mesh=mesh, in_specs=in_specs, out_specs=out_specs, check_vma=False
    )
```

```python
import functools

import jax
import jax.numpy as jnp
from jax import lax
from jax.experimental import pallas as pl
from jax.experimental.pallas import tpu as pltpu
from jax.sharding import PartitionSpec as P

NOPE = 128
ROPE = 64
LAT = 512
PAGE = 128
LANES = 128
LAT_TILES = LAT // LANES
LOG2E = 1.4426950408889634
SOFTMAX_SCALE = (NOPE + ROPE) ** (-0.5)
LOWEST = -1e30
STAT_ROWS = 16


def head_of_row(shape, heads):
    return lax.rem(lax.broadcasted_iota(jnp.int32, shape, 0), heads)


def query_kernel(queries_hbm, absorb_hbm, out_ref, again_ref, queries_ref, absorb_ref, sems):
    rows = queries_ref.shape[0]
    heads = absorb_ref.shape[0]
    half = rows // 2
    pieces = sems.shape[0] - 1
    group = heads // pieces
    copies = [pltpu.make_async_copy(queries_hbm, queries_ref, sems.at[pieces])] + [
        pltpu.make_async_copy(
            absorb_hbm.at[pl.ds(i * group, group)],
            absorb_ref.at[pl.ds(i * group, group)],
            sems.at[i],
        )
        for i in range(pieces)
    ]
    for copy in copies:
        copy.start()
    copies[0].wait()
    nope = queries_ref[:, :NOPE]
    owner = head_of_row((rows, NOPE), heads)
    latent = jnp.zeros((rows, LAT), jnp.float32)
    for i in range(pieces):
        spread = jnp.concatenate(
            [
                jnp.where(owner == h, nope, jnp.zeros_like(nope))
                for h in range(i * group, (i + 1) * group)
            ],
            axis=1,
        )
        copies[i + 1].wait()
        latent += jnp.dot(
            spread,
            absorb_ref[i * group : (i + 1) * group].reshape(group * NOPE, LAT),
            preferred_element_type=jnp.float32,
        )
    latent = latent.astype(jnp.bfloat16)
    rope = queries_ref[:, NOPE:]
    rope = jnp.concatenate([rope[:half], rope[half:]], axis=1)
    for b in range(2):
        for j in range(LAT_TILES):
            start = (b * LAT_TILES + j) * half
            out_ref[start : start + half, :] = latent[
                b * half : (b + 1) * half, j * LANES : (j + 1) * LANES
            ]
    out_ref[2 * LAT_TILES * half :, :] = rope
    again_ref[...] = out_ref[...]


def lanes_kernel(rate_ref, scale_ref, through_ref, inv_rate_ref, scales_ref, passed_ref, *, ctx):
    del through_ref, passed_ref
    line = ctx // 2
    me = lax.axis_index("ctx")
    for source, target in ((1.0 / rate_ref[...], inv_rate_ref), (scale_ref[...], scales_ref)):
        size = source.shape[1]
        heads = size // ctx
        same = lax.broadcasted_iota(jnp.int32, (size, size), 0) == lax.broadcasted_iota(
            jnp.int32, (size, size), 1
        )
        column = jnp.sum(jnp.where(same, source, 0.0), axis=1, keepdims=True)
        column = jnp.broadcast_to(column, (size, LANES)).reshape(ctx, heads, LANES)
        rows = []
        for k in range(ctx):
            owner = me ^ (2 * (k % line) + k // line)
            picked = jnp.zeros((heads, LANES), jnp.float32)
            for device in range(ctx):
                picked = jnp.where(owner == device, column[device], picked)
            rows.append(picked)
        target[...] = jnp.concatenate(rows, axis=0).T[: target.shape[0]]


def turn_kernel(cache_ref, out_ref, *, b):
    width = 2 * PAGE
    for i in range(out_ref.shape[0] // width):
        at = slice(i * width, (i + 1) * width)
        out_ref[at, :] = cache_ref[b, :, at].T


def attention_kernel(pages_ref, lengths_ref, *refs, ctx, b):
    query_refs, refs = refs[:ctx], refs[ctx:]
    cache_ref, turned_ref, inv_rate, scale, near_ref, far_ref, query, held, acc, *buffers = refs
    scores_of, weights_of, factor_of = buffers[:2], buffers[2:4], buffers[4:]
    chunk, rows = scores_of[0].shape
    half = rows // ctx
    heads = half // 2
    line = ctx // 2
    steps = cache_ref.shape[2] // chunk
    group = 4
    group_width = group * PAGE
    groups = chunk // group_width
    request_rows = LAT_TILES * half
    start = b * request_rows

    side = rows // 2
    for k, block in enumerate(query_refs):
        for q in range(2):
            own = slice(q * side + k * heads, q * side + (k + 1) * heads)
            for j in range(LAT_TILES):
                at = start + j * half + q * heads
                query[own, j * LANES : (j + 1) * LANES] = block[at : at + heads, :]
            at = 2 * request_rows + q * heads
            query[own, LAT:] = block[at : at + heads, b * ROPE : (b + 1) * ROPE]

    held[...] = query[...].T
    first_pos = lengths_ref[b] - 2
    own_rate, own_scale = inv_rate[0:1, :], scale[0:1, :]
    back = lax.broadcasted_iota(jnp.int32, (PAGE + 8, side), 0).astype(jnp.float32)

    def raw_scores(at):
        return jnp.dot(
            turned_ref[at * group_width : (at + 1) * group_width, :],
            held[...],
            preferred_element_type=jnp.float32,
        )

    def add_products(step):
        weights, factor = weights_of[step % 2], factor_of[step % 2]
        for at in (slice(0, LAT // 2), slice(LAT // 2, LAT)):
            new = jnp.dot(
                cache_ref[b, at, step * chunk : (step + 1) * chunk],
                weights[...],
                preferred_element_type=jnp.float32,
            )
            acc[at, :] = acc[at, :] * factor[0:1, :] + new if step else new

    top = jnp.full((1, rows), LOWEST, jnp.float32)
    total = jnp.zeros((1, rows), jnp.float32)
    ahead = raw_scores(0)
    for step in range(steps):
        scores, weights = scores_of[step % 2], weights_of[step % 2]
        tops = jnp.full((8, rows), LOWEST, jnp.float32)
        for piece in range(groups):
            raw = ahead
            at = step * groups + piece
            if at + 1 < steps * groups:
                ahead = raw_scores(at + 1)
            for side_of in range(group):
                page = piece * group + side_of
                base = first_pos - pages_ref[b, step * (chunk // PAGE) + page] * PAGE
                reach = (base + 1).astype(jnp.float32) - back
                spread = jnp.where(reach >= 0.0, reach, jnp.inf)
                bias = own_scale * jnp.log2(spread + own_rate)
                value = raw[side_of * PAGE : (side_of + 1) * PAGE] * (
                    SOFTMAX_SCALE * LOG2E
                ) - jnp.concatenate([bias[1 : PAGE + 1], bias[:PAGE]], axis=1)
                tops = jnp.maximum(tops, jnp.max(value.reshape(PAGE // 8, 8, rows), axis=0))
                scores[page * PAGE : (page + 1) * PAGE, :] = value
        before = top
        top = jnp.maximum(before, jnp.max(tops, axis=0, keepdims=True))
        factor = jnp.exp2(before - top)
        factor_of[step % 2][...] = jnp.broadcast_to(factor, (8, rows))
        if step:
            add_products(step - 1)
        sums = jnp.zeros((8, rows), jnp.float32)
        for page in range(chunk // PAGE):
            at = slice(page * PAGE, (page + 1) * PAGE)
            value = jnp.exp2(scores[at, :] - top)
            sums += jnp.sum(value.reshape(PAGE // 8, 8, rows), axis=0)
            weights[at, :] = value.astype(jnp.bfloat16)
        total = total * factor + jnp.sum(sums, axis=0, keepdims=True)
    add_products(steps - 1)

    seen = total > 0.0
    safe = jnp.where(seen, total, 1.0)
    share = 1.0 / safe
    logs = jnp.where(seen, top + jnp.log2(safe), LOWEST)
    logs = jnp.broadcast_to(logs, (LANES, rows))
    turned = []
    for q in range(2):
        at = slice(q * side, (q + 1) * side)
        turned.append(logs[:, at].T.reshape(ctx, heads, LANES))
        for j in range(LAT_TILES):
            part = (acc[j * LANES : (j + 1) * LANES, at] * share[:, at]).T
            part = part.astype(jnp.bfloat16).reshape(ctx, heads, LANES)
            first = j * half + q * heads
            near_ref[:, first : first + heads, :] = part[:line]
            far_ref[:, first : first + heads, :] = part[line:]
    log_total = jnp.concatenate(turned, axis=1)
    across = jnp.sum(jnp.where(diagonal(half), log_total, 0.0), axis=1, keepdims=True)
    packed = three_parts(across).astype(jnp.bfloat16)
    near_ref[:, request_rows:, :] = packed[:line]
    far_ref[:, request_rows:, :] = packed[line:]


def diagonal(half):
    return lax.broadcasted_iota(jnp.int32, (half, LANES), 0) == lax.broadcasted_iota(
        jnp.int32, (half, LANES), 1
    )


def three_parts(value):
    high = value.astype(jnp.bfloat16).astype(jnp.float32)
    middle = (value - high).astype(jnp.bfloat16).astype(jnp.float32)
    low = value - high - middle
    row = lax.broadcasted_iota(jnp.int32, (value.shape[0], STAT_ROWS, LANES), 1)
    return jnp.where(
        row == 0, high, jnp.where(row == 1, middle, jnp.where(row == 2, low, 0.0))
    )


def logs_of(stats):
    return jnp.sum(stats.astype(jnp.float32), axis=1, keepdims=True)


def as_column(across, half):
    return jnp.sum(jnp.where(diagonal(half), across, 0.0), axis=-1, keepdims=True)


def merge_kernel(own_ref, other_ref, *out_refs):
    request_rows = own_ref.shape[1] - STAT_ROWS
    half = request_rows // LAT_TILES
    own_log = logs_of(own_ref[:, request_rows:, :])
    other_log = logs_of(other_ref[:, request_rows:, :])
    high = jnp.maximum(own_log, other_log)
    own_factor = jnp.exp2(own_log - high)
    other_factor = jnp.exp2(other_log - high)
    both = own_factor + other_factor
    stats = three_parts(high + jnp.log2(both)).astype(jnp.bfloat16)
    own_factor = as_column(own_factor / both, half)
    other_factor = as_column(other_factor / both, half)
    for j in range(LAT_TILES):
        at = slice(j * half, (j + 1) * half)
        merged = (
            own_ref[:, at, :].astype(jnp.float32) * own_factor
            + other_ref[:, at, :].astype(jnp.float32) * other_factor
        ).astype(jnp.bfloat16)
        for k, out_ref in enumerate(out_refs):
            out_ref[at, :] = merged[k]
    for k, out_ref in enumerate(out_refs):
        out_ref[request_rows:, :] = stats[k]


def output_kernel(*refs):
    *part_refs, up_ref, weight_ref, out_ref, values, attn = refs
    heads = up_ref.shape[0]
    half = 2 * heads
    rows = 2 * half
    request_rows = LAT_TILES * half
    for b in range(2):
        parts = part_refs[b * len(part_refs) // 2 : (b + 1) * len(part_refs) // 2]
        logs = logs_of(jnp.stack([part[request_rows:, :] for part in parts]))
        factor = jnp.exp2(logs - jnp.max(logs, axis=0, keepdims=True))
        factor = as_column(factor / jnp.sum(factor, axis=0, keepdims=True), half)
        for j in range(LAT_TILES):
            at = slice(j * half, (j + 1) * half)
            attn[b * half : (b + 1) * half, j * LANES : (j + 1) * LANES] = sum(
                part[at, :].astype(jnp.float32) * factor[k] for k, part in enumerate(parts)
            ).astype(jnp.bfloat16)
    latent = attn[...]
    owner = head_of_row(latent.shape, heads)
    up = jnp.zeros((rows, up_ref.shape[2]), jnp.float32)
    for h in range(heads):
        own = jnp.where(owner == h, latent, jnp.zeros_like(latent))
        up += jnp.dot(own, up_ref[h], preferred_element_type=jnp.float32)
    up = up.astype(jnp.bfloat16)
    owner = head_of_row(up.shape, heads)
    spread = jnp.concatenate(
        [jnp.where(owner == h, up, jnp.zeros_like(up)) for h in range(heads)], axis=1
    )
    token = lax.broadcasted_iota(jnp.int32, (8, rows), 0)
    group = lax.broadcasted_iota(jnp.int32, (8, rows), 1) // heads
    pick = jnp.where(token == group, 1.0, 0.0).astype(jnp.bfloat16)
    values[...] = jnp.dot(pick, spread, preferred_element_type=jnp.float32)
    project(values, weight_ref, out_ref, True)


def project(values, weight_ref, out_ref, far):
    blocks, tokens, width = out_ref.shape
    bit = lax.rem(lax.axis_index("ctx") // 2, 2)
    first = (1 - bit if far else bit) * (2 * width)

    @pl.loop(0, blocks // 2)
    def _(k):
        result = jnp.dot(
            values[...].astype(jnp.bfloat16),
            weight_ref[:, pl.ds(pl.multiple_of(first + k * (4 * width), LANES), 2 * width)],
            preferred_element_type=jnp.float32,
        )
        out_ref[2 * k] = result[:tokens, :width].astype(out_ref.dtype)
        out_ref[2 * k + 1] = result[:tokens, width:].astype(out_ref.dtype)


def near_kernel(values, weight_ref, out_ref):
    project(values, weight_ref, out_ref, False)


def add_kernel(own_ref, other_ref, kept_ref, *sent_refs):
    me = lax.axis_index("ctx")
    own = (me // 4) * 2 + lax.rem(me, 2)
    for k, out_ref in enumerate((kept_ref,) + sent_refs):
        block = own_ref[own ^ k] + other_ref[own ^ k].astype(jnp.float32)
        out_ref[...] = block.astype(out_ref.dtype)


def sum_kernel(own_ref, *refs):
    *other_refs, out_ref = refs
    result = own_ref[...]
    for other in other_refs:
        result += other[...].astype(jnp.float32)
    requests, tokens, _ = out_ref.shape
    for b in range(requests):
        out_ref[b] = result[b * tokens : (b + 1) * tokens].astype(out_ref.dtype)


def per_device(
    queries,
    key_absorb,
    latent_cache,
    page_order,
    lengths,
    kerple_scale,
    kerple_rate,
    value_up,
    output_weight,
    *,
    ctx,
):
    requests, query_len, heads, query_width = queries.shape
    keys_dev = latent_cache.shape[1]
    half = query_len * heads
    rows = requests * half
    request_rows = LAT_TILES * half
    width = output_weight.shape[1] // ctx
    chunk = 1024

    hint = pl.CostEstimate(flops=20 * 10**9, bytes_accessed=2**20, transcendentals=0)
    long_hint = pl.CostEstimate(flops=100 * 10**9, bytes_accessed=2**20, transcendentals=0)
    in_hbm = lambda value: pltpu.with_memory_space_constraint(value, pltpu.HBM)
    in_vmem = lambda value: pltpu.with_memory_space_constraint(value, pltpu.VMEM)
    line = ctx // 2
    swap = lambda value, bits: lax.ppermute(value, "ctx", [(i, i ^ bits) for i in range(ctx)])
    packed, again = pl.pallas_call(
        query_kernel,
        in_specs=[pl.BlockSpec(memory_space=pl.ANY)] * 2,
        out_shape=[jax.ShapeDtypeStruct((2 * request_rows + half, LANES), jnp.bfloat16)] * 2,
        scratch_shapes=[
            pltpu.VMEM((rows, query_width), jnp.bfloat16),
            pltpu.VMEM(key_absorb.shape, jnp.bfloat16),
            pltpu.SemaphoreType.DMA((5,)),
        ],
        compiler_params=pltpu.CompilerParams(vmem_limit_bytes=8 * 2**20),
        name="latent_query",
    )(in_hbm(queries.reshape(rows, query_width)), in_hbm(key_absorb))
    by_row = (8, ctx * heads)
    inv_rate, scale, again = pl.pallas_call(
        functools.partial(lanes_kernel, ctx=ctx),
        in_specs=[pl.BlockSpec(memory_space=pltpu.VMEM)] * 2
        + [pl.BlockSpec(memory_space=pl.ANY)],
        out_specs=[pl.BlockSpec(memory_space=pltpu.VMEM)] * 2
        + [pl.BlockSpec(memory_space=pl.ANY)],
        out_shape=[jax.ShapeDtypeStruct(by_row, jnp.float32)] * 2
        + [jax.ShapeDtypeStruct(again.shape, again.dtype)],
        input_output_aliases={2: 2},
        compiler_params=pltpu.CompilerParams(vmem_limit_bytes=4 * 2**20),
        name="head_lanes",
        cost_estimate=long_hint,
    )(in_hbm(kerple_rate.reshape(1, -1)), in_hbm(kerple_scale.reshape(1, -1)), again)
    column = [packed] + [swap(packed, 2 * k) for k in range(1, line)]
    gathered = column + [swap(value, 1) for value in [again] + column[1:]]

    cache = in_vmem(jnp.swapaxes(latent_cache, 1, 2))
    turned = [
        pl.pallas_call(
            functools.partial(turn_kernel, b=b),
            out_shape=jax.ShapeDtypeStruct((keys_dev, LAT + ROPE), jnp.bfloat16),
            compiler_params=pltpu.CompilerParams(vmem_limit_bytes=4 * 2**20),
            name="turn_cache",
        )(cache)
        for b in range(requests)
    ]
    all_rows = ctx * half
    message = (request_rows + STAT_ROWS, LANES)
    in_smem = pl.BlockSpec(memory_space=pltpu.SMEM)
    whole = pl.BlockSpec(memory_space=pltpu.VMEM)
    parts = []
    for b in range(requests):
        near, far = pl.pallas_call(
            functools.partial(attention_kernel, ctx=ctx, b=b),
            in_specs=[in_smem, in_smem] + [whole] * (ctx + 4),
            out_shape=[jax.ShapeDtypeStruct((line,) + message, jnp.bfloat16)] * 2,
            scratch_shapes=[
                pltpu.VMEM((all_rows, LAT + ROPE), jnp.bfloat16),
                pltpu.VMEM((LAT + ROPE, all_rows), jnp.bfloat16),
                pltpu.VMEM((LAT, all_rows), jnp.float32),
            ]
            + [pltpu.VMEM((chunk, all_rows), jnp.float32)] * 2
            + [pltpu.VMEM((chunk, all_rows), jnp.bfloat16)] * 2
            + [pltpu.VMEM((8, all_rows), jnp.float32)] * 2,
            compiler_params=pltpu.CompilerParams(vmem_limit_bytes=8 * 2**20),
            cost_estimate=hint,
            name="attention",
        )(in_hbm(page_order), in_hbm(lengths), *gathered, cache, in_vmem(turned[b]), inv_rate, scale)
        merged = pl.pallas_call(
            merge_kernel,
            out_shape=[jax.ShapeDtypeStruct(message, jnp.bfloat16) for _ in range(line)],
            compiler_params=pltpu.CompilerParams(vmem_limit_bytes=4 * 2**20),
            name="merge",
        )(near, swap(far, 1))
        parts.append(merged[0])
        parts += [swap(merged[k], 2 * k) for k in range(1, line)]

    tokens = requests * query_len
    weight = in_vmem(output_weight)
    small = pltpu.CompilerParams(vmem_limit_bytes=4 * 2**20)
    far, values = pl.pallas_call(
        output_kernel,
        out_shape=[
            jax.ShapeDtypeStruct((line, tokens, width), jnp.bfloat16),
            jax.ShapeDtypeStruct((8, output_weight.shape[0]), jnp.float32),
        ],
        scratch_shapes=[pltpu.VMEM((rows, LAT), jnp.bfloat16)],
        compiler_params=small,
        cost_estimate=hint,
        name="up_and_far_output",
    )(*parts, in_vmem(value_up), weight)
    near = pl.pallas_call(
        near_kernel,
        out_shape=jax.ShapeDtypeStruct((line, tokens, width), jnp.float32),
        compiler_params=small,
        cost_estimate=hint,
        name="near_output",
    )(values, weight)
    block = (tokens, width)
    kept, *sent = pl.pallas_call(
        add_kernel,
        out_shape=[jax.ShapeDtypeStruct(block, jnp.float32)]
        + [jax.ShapeDtypeStruct(block, jnp.bfloat16)] * 3,
        compiler_params=small,
        name="add_columns",
    )(near, swap(far, 2))
    return pl.pallas_call(
        sum_kernel,
        out_shape=jax.ShapeDtypeStruct((requests, query_len, width), jnp.bfloat16),
        compiler_params=small,
        name="sum_output",
    )(kept, *(swap(part, bits) for part, bits in zip(sent, (1, 4, 5))))


def plain_device(
    queries,
    key_absorb,
    latent_cache,
    page_order,
    lengths,
    kerple_scale,
    kerple_rate,
    value_up,
    output_weight,
    *,
    ctx,
):
    requests, query_len, heads, _ = queries.shape
    width = output_weight.shape[1] // ctx
    latent_query = jnp.einsum(
        "bqhn,hnc->bqhc", queries[..., :NOPE], key_absorb, preferred_element_type=jnp.float32
    ).astype(jnp.bfloat16)
    own_query = jnp.concatenate([latent_query, queries[..., NOPE:]], axis=-1)
    full_query = lax.all_gather(own_query, "ctx", axis=2, tiled=True)
    offsets = jnp.arange(PAGE, dtype=jnp.int32)
    key_pos = (page_order[:, :, None] * PAGE + offsets).reshape(requests, -1)
    query_pos = lengths[:, None] - query_len + jnp.arange(query_len, dtype=jnp.int32)
    distance = query_pos[:, :, None] - key_pos[:, None, :]
    visible = (distance >= 0)[:, :, None, :]
    spread = jnp.maximum(distance, 0).astype(jnp.float32)[:, :, None, :]
    log_bias = kerple_scale[:, None] * jnp.log(1.0 + kerple_rate[:, None] * spread)
    scores = jnp.einsum(
        "bqhc,btc->bqht", full_query, latent_cache, preferred_element_type=jnp.float32
    )
    scores = jnp.where(visible, scores * SOFTMAX_SCALE - log_bias, LOWEST)
    row_max = jnp.max(scores, axis=-1)
    weights = jnp.where(visible, jnp.exp(scores - row_max[..., None]), 0.0)
    summed = jnp.einsum(
        "bqht,btc->bqhc",
        weights.astype(jnp.bfloat16),
        latent_cache[..., :LAT],
        preferred_element_type=jnp.float32,
    )
    factor = jnp.exp(row_max - lax.pmax(row_max, "ctx"))
    shared_total = lax.psum_scatter(
        jnp.sum(weights, axis=-1) * factor, "ctx", scatter_dimension=2, tiled=True
    )
    shared_sum = lax.psum_scatter(
        summed * factor[..., None], "ctx", scatter_dimension=2, tiled=True
    )
    attn_latent = (shared_sum / shared_total[..., None]).astype(jnp.bfloat16)
    up_values = jnp.einsum(
        "bqhc,hcv->bqhv", attn_latent, value_up, preferred_element_type=jnp.float32
    ).astype(jnp.bfloat16)
    partial_out = jnp.dot(
        up_values.reshape(requests * query_len, -1),
        output_weight,
        preferred_element_type=jnp.float32,
    )
    summed_out = lax.psum_scatter(partial_out, "ctx", scatter_dimension=1, tiled=True)
    return summed_out.astype(jnp.bfloat16).reshape(requests, query_len, width)


def solution(mesh):
    ctx = mesh.shape["ctx"]
    in_specs = (
        P("rep", None, "ctx", None),
        P("ctx", None, None),
        P("rep", "ctx", None),
        P("rep", "ctx"),
        P("rep"),
        P(),
        P(),
        P("ctx", None, None),
        P("ctx", None),
    )
    out_specs = P("rep", None, "ctx")

    def device_program(*args):
        heads = args[0].shape[2]
        width = args[-1].shape[1] // ctx
        tiled = ctx == 8 and ctx * heads == LANES and width % LANES == 0
        return (per_device if tiled else plain_device)(*args, ctx=ctx)

    return jax.shard_map(
        device_program, mesh=mesh, in_specs=in_specs, out_specs=out_specs, check_vma=False
    )
```

```python
import functools

import jax
import jax.numpy as jnp
from jax import lax
from jax.experimental import pallas as pl
from jax.experimental.pallas import tpu as pltpu
from jax.sharding import PartitionSpec as P

NOPE = 128
ROPE = 64
LAT = 512
PAGE = 128
LANES = 128
LAT_TILES = LAT // LANES
LOG2E = 1.4426950408889634
SOFTMAX_SCALE = (NOPE + ROPE) ** (-0.5)
LOWEST = -1e30
STAT_ROWS = 16


def head_of_row(shape, heads):
    return lax.rem(lax.broadcasted_iota(jnp.int32, shape, 0), heads)


def query_kernel(queries_hbm, absorb_hbm, out_ref, again_ref, queries_ref, absorb_ref, sems):
    rows = queries_ref.shape[0]
    heads = absorb_ref.shape[0]
    half = rows // 2
    pieces = sems.shape[0] - 1
    group = heads // pieces
    copies = [pltpu.make_async_copy(queries_hbm, queries_ref, sems.at[pieces])] + [
        pltpu.make_async_copy(
            absorb_hbm.at[pl.ds(i * group, group)],
            absorb_ref.at[pl.ds(i * group, group)],
            sems.at[i],
        )
        for i in range(pieces)
    ]
    for copy in copies:
        copy.start()
    copies[0].wait()
    nope = queries_ref[:, :NOPE]
    owner = head_of_row((rows, NOPE), heads)
    latent = jnp.zeros((rows, LAT), jnp.float32)
    for i in range(pieces):
        spread = jnp.concatenate(
            [
                jnp.where(owner == h, nope, jnp.zeros_like(nope))
                for h in range(i * group, (i + 1) * group)
            ],
            axis=1,
        )
        copies[i + 1].wait()
        latent += jnp.dot(
            spread,
            absorb_ref[i * group : (i + 1) * group].reshape(group * NOPE, LAT),
            preferred_element_type=jnp.float32,
        )
    latent = latent.astype(jnp.bfloat16)
    rope = queries_ref[:, NOPE:]
    rope = jnp.concatenate([rope[:half], rope[half:]], axis=1)
    for b in range(2):
        for j in range(LAT_TILES):
            start = (b * LAT_TILES + j) * half
            out_ref[start : start + half, :] = latent[
                b * half : (b + 1) * half, j * LANES : (j + 1) * LANES
            ]
    out_ref[2 * LAT_TILES * half :, :] = rope
    again_ref[...] = out_ref[...]


def column_kernel(rate_ref, scale_ref, through_ref, inv_rate_ref, scales_ref, passed_ref):
    del through_ref, passed_ref
    ctx, heads, _ = inv_rate_ref.shape
    line = ctx // 2
    me = lax.axis_index("ctx")
    for source, target in ((1.0 / rate_ref[...], inv_rate_ref), (scale_ref[...], scales_ref)):
        size = source.shape[1]
        same = lax.broadcasted_iota(jnp.int32, (size, size), 0) == lax.broadcasted_iota(
            jnp.int32, (size, size), 1
        )
        column = jnp.sum(jnp.where(same, source, 0.0), axis=1, keepdims=True)
        column = jnp.broadcast_to(column, (size, LANES)).reshape(ctx, heads, LANES)
        for k in range(ctx):
            owner = me ^ (2 * (k % line) + k // line)
            picked = jnp.zeros((heads, LANES), jnp.float32)
            for device in range(ctx):
                picked = jnp.where(owner == device, column[device], picked)
            target[k] = picked


def attention_kernel(pages_ref, lengths_ref, *refs, ctx, b):
    query_refs, refs = refs[:ctx], refs[ctx:]
    cache_ref, inv_rate, scale, near_ref, far_ref, query, acc, total, *buffers = refs
    scores_of, weights_of, factor_of = buffers[:2], buffers[2:4], buffers[4:]
    rows, chunk = scores_of[0].shape
    half = rows // ctx
    heads = half // 2
    line = ctx // 2
    steps = cache_ref.shape[2] // chunk
    pair_width = 2 * PAGE
    pairs = chunk // pair_width
    request_rows = LAT_TILES * half
    start = b * request_rows

    for k, block in enumerate(query_refs):
        own = slice(k * half, (k + 1) * half)
        for j in range(LAT_TILES):
            query[own, j * LANES : (j + 1) * LANES] = block[
                start + j * half : start + (j + 1) * half, :
            ]
        query[own, LAT:] = block[2 * request_rows :, b * ROPE : (b + 1) * ROPE]

    lane = lax.broadcasted_iota(jnp.int32, (heads, LANES), 1)
    first_pos = lengths_ref[b] - 2

    def raw_scores(at):
        return jnp.dot(
            query[...],
            cache_ref[b, :, at * pair_width : (at + 1) * pair_width],
            preferred_element_type=jnp.float32,
        )

    def add_products(step):
        weights, factor = weights_of[step % 2], factor_of[step % 2]
        for columns in (slice(0, LAT // 2), slice(LAT // 2, LAT)):
            new = lax.dot_general(
                weights[...],
                cache_ref[b, columns, step * chunk : (step + 1) * chunk],
                (((1,), (1,)), ((), ())),
                preferred_element_type=jnp.float32,
            )
            for j in range(columns.start, columns.stop, LANES):
                part = new[:, j - columns.start : j - columns.start + LANES]
                at = slice(j, j + LANES)
                acc[:, at] = acc[:, at] * factor[...] + part if step else part

    top = jnp.full((rows, LANES), LOWEST, jnp.float32)
    ahead = raw_scores(0)
    for step in range(steps):
        scores, weights = scores_of[step % 2], weights_of[step % 2]
        tops = [None, None]
        for pair in range(pairs):
            raw = ahead
            at = step * pairs + pair
            if at + 1 < steps * pairs:
                ahead = raw_scores(at + 1)
            for side in range(2):
                page = pair * 2 + side
                columns = slice(page * PAGE, (page + 1) * PAGE)
                part = raw[:, side * PAGE : (side + 1) * PAGE].reshape(ctx, 2, heads, PAGE)
                base = first_pos - pages_ref[b, step * (chunk // PAGE) + page] * PAGE
                values = []
                for q in range(2):
                    distance = base + q - lane
                    spread = jnp.where(distance >= 0, distance.astype(jnp.float32), jnp.inf)
                    logs = jnp.log2(spread[None] + inv_rate[...])
                    value = part[:, q] * (SOFTMAX_SCALE * LOG2E) - scale[...] * logs
                    tops[q] = value if tops[q] is None else jnp.maximum(tops[q], value)
                    values.append(value)
                scores[:, columns] = jnp.stack(values, axis=1).reshape(rows, PAGE)
        lane_top = jnp.stack(tops, axis=1).reshape(rows, LANES)
        before = top
        top = jnp.maximum(before, jnp.max(lane_top, axis=1, keepdims=True))
        factor = jnp.exp2(before - top)
        factor_of[step % 2][...] = factor
        if step:
            add_products(step - 1)
        lane_total = total[...] * factor if step else jnp.zeros((rows, LANES), jnp.float32)
        for page in range(chunk // PAGE):
            columns = slice(page * PAGE, (page + 1) * PAGE)
            value = jnp.exp2(scores[:, columns] - top)
            lane_total += value
            weights[:, columns] = value.astype(jnp.bfloat16)
        total[...] = lane_total
    add_products(steps - 1)

    row_total = jnp.sum(total[...], axis=1, keepdims=True)
    row_total = jnp.broadcast_to(row_total, (rows, LANES))
    seen = row_total > 0.0
    safe = jnp.where(seen, row_total, 1.0)
    share = 1.0 / safe
    for j in range(LAT_TILES):
        columns = slice(j * LANES, (j + 1) * LANES)
        part = (acc[:, columns] * share).astype(jnp.bfloat16).reshape(ctx, half, LANES)
        near_ref[:, j * half : (j + 1) * half, :] = part[:line]
        far_ref[:, j * half : (j + 1) * half, :] = part[line:]
    log_total = jnp.where(seen, top + jnp.log2(safe), LOWEST).reshape(ctx, half, LANES)
    across = jnp.sum(jnp.where(diagonal(half), log_total, 0.0), axis=1, keepdims=True)
    packed = three_parts(across).astype(jnp.bfloat16)
    near_ref[:, request_rows:, :] = packed[:line]
    far_ref[:, request_rows:, :] = packed[line:]


def diagonal(half):
    return lax.broadcasted_iota(jnp.int32, (half, LANES), 0) == lax.broadcasted_iota(
        jnp.int32, (half, LANES), 1
    )


def three_parts(value):
    high = value.astype(jnp.bfloat16).astype(jnp.float32)
    middle = (value - high).astype(jnp.bfloat16).astype(jnp.float32)
    low = value - high - middle
    row = lax.broadcasted_iota(jnp.int32, (value.shape[0], STAT_ROWS, LANES), 1)
    return jnp.where(
        row == 0, high, jnp.where(row == 1, middle, jnp.where(row == 2, low, 0.0))
    )


def logs_of(stats):
    return jnp.sum(stats.astype(jnp.float32), axis=1, keepdims=True)


def as_column(across, half):
    return jnp.sum(jnp.where(diagonal(half), across, 0.0), axis=-1, keepdims=True)


def merge_kernel(own_ref, other_ref, *out_refs):
    request_rows = own_ref.shape[1] - STAT_ROWS
    half = request_rows // LAT_TILES
    own_log = logs_of(own_ref[:, request_rows:, :])
    other_log = logs_of(other_ref[:, request_rows:, :])
    high = jnp.maximum(own_log, other_log)
    own_factor = jnp.exp2(own_log - high)
    other_factor = jnp.exp2(other_log - high)
    both = own_factor + other_factor
    stats = three_parts(high + jnp.log2(both)).astype(jnp.bfloat16)
    own_factor = as_column(own_factor / both, half)
    other_factor = as_column(other_factor / both, half)
    for j in range(LAT_TILES):
        at = slice(j * half, (j + 1) * half)
        merged = (
            own_ref[:, at, :].astype(jnp.float32) * own_factor
            + other_ref[:, at, :].astype(jnp.float32) * other_factor
        ).astype(jnp.bfloat16)
        for k, out_ref in enumerate(out_refs):
            out_ref[at, :] = merged[k]
    for k, out_ref in enumerate(out_refs):
        out_ref[request_rows:, :] = stats[k]


def output_kernel(*refs):
    *part_refs, up_ref, weight_ref, out_ref, values, attn = refs
    heads = up_ref.shape[0]
    half = 2 * heads
    rows = 2 * half
    request_rows = LAT_TILES * half
    for b in range(2):
        parts = part_refs[b * len(part_refs) // 2 : (b + 1) * len(part_refs) // 2]
        logs = logs_of(jnp.stack([part[request_rows:, :] for part in parts]))
        factor = jnp.exp2(logs - jnp.max(logs, axis=0, keepdims=True))
        factor = as_column(factor / jnp.sum(factor, axis=0, keepdims=True), half)
        for j in range(LAT_TILES):
            at = slice(j * half, (j + 1) * half)
            attn[b * half : (b + 1) * half, j * LANES : (j + 1) * LANES] = sum(
                part[at, :].astype(jnp.float32) * factor[k] for k, part in enumerate(parts)
            ).astype(jnp.bfloat16)
    latent = attn[...]
    owner = head_of_row(latent.shape, heads)
    up = jnp.zeros((rows, up_ref.shape[2]), jnp.float32)
    for h in range(heads):
        own = jnp.where(owner == h, latent, jnp.zeros_like(latent))
        up += jnp.dot(own, up_ref[h], preferred_element_type=jnp.float32)
    up = up.astype(jnp.bfloat16)
    owner = head_of_row(up.shape, heads)
    spread = jnp.concatenate(
        [jnp.where(owner == h, up, jnp.zeros_like(up)) for h in range(heads)], axis=1
    )
    token = lax.broadcasted_iota(jnp.int32, (8, rows), 0)
    group = lax.broadcasted_iota(jnp.int32, (8, rows), 1) // heads
    pick = jnp.where(token == group, 1.0, 0.0).astype(jnp.bfloat16)
    values[...] = jnp.dot(pick, spread, preferred_element_type=jnp.float32)
    project(values, weight_ref, out_ref, True)


def project(values, weight_ref, out_ref, far):
    blocks, tokens, width = out_ref.shape
    bit = lax.rem(lax.axis_index("ctx") // 2, 2)
    first = (1 - bit if far else bit) * (2 * width)

    @pl.loop(0, blocks // 2)
    def _(k):
        result = jnp.dot(
            values[...].astype(jnp.bfloat16),
            weight_ref[:, pl.ds(pl.multiple_of(first + k * (4 * width), LANES), 2 * width)],
            preferred_element_type=jnp.float32,
        )
        out_ref[2 * k] = result[:tokens, :width].astype(out_ref.dtype)
        out_ref[2 * k + 1] = result[:tokens, width:].astype(out_ref.dtype)


def near_kernel(values, weight_ref, out_ref):
    project(values, weight_ref, out_ref, False)


def add_kernel(own_ref, other_ref, kept_ref, *sent_refs):
    me = lax.axis_index("ctx")
    own = (me // 4) * 2 + lax.rem(me, 2)
    for k, out_ref in enumerate((kept_ref,) + sent_refs):
        block = own_ref[own ^ k] + other_ref[own ^ k].astype(jnp.float32)
        out_ref[...] = block.astype(out_ref.dtype)


def sum_kernel(own_ref, *refs):
    *other_refs, out_ref = refs
    result = own_ref[...]
    for other in other_refs:
        result += other[...].astype(jnp.float32)
    requests, tokens, _ = out_ref.shape
    for b in range(requests):
        out_ref[b] = result[b * tokens : (b + 1) * tokens].astype(out_ref.dtype)


def per_device(
    queries,
    key_absorb,
    latent_cache,
    page_order,
    lengths,
    kerple_scale,
    kerple_rate,
    value_up,
    output_weight,
    *,
    ctx,
):
    requests, query_len, heads, query_width = queries.shape
    keys_dev = latent_cache.shape[1]
    half = query_len * heads
    rows = requests * half
    request_rows = LAT_TILES * half
    width = output_weight.shape[1] // ctx
    chunk = 1024

    hint = pl.CostEstimate(flops=20 * 10**9, bytes_accessed=2**20, transcendentals=0)
    long_hint = pl.CostEstimate(flops=100 * 10**9, bytes_accessed=2**20, transcendentals=0)
    in_hbm = lambda value: pltpu.with_memory_space_constraint(value, pltpu.HBM)
    in_vmem = lambda value: pltpu.with_memory_space_constraint(value, pltpu.VMEM)
    line = ctx // 2
    swap = lambda value, bits: lax.ppermute(value, "ctx", [(i, i ^ bits) for i in range(ctx)])
    packed, again = pl.pallas_call(
        query_kernel,
        in_specs=[pl.BlockSpec(memory_space=pl.ANY)] * 2,
        out_shape=[jax.ShapeDtypeStruct((2 * request_rows + half, LANES), jnp.bfloat16)] * 2,
        scratch_shapes=[
            pltpu.VMEM((rows, query_width), jnp.bfloat16),
            pltpu.VMEM(key_absorb.shape, jnp.bfloat16),
            pltpu.SemaphoreType.DMA((5,)),
        ],
        compiler_params=pltpu.CompilerParams(vmem_limit_bytes=8 * 2**20),
        name="latent_query",
    )(in_hbm(queries.reshape(rows, query_width)), in_hbm(key_absorb))
    columns = (ctx, heads, LANES)
    inv_rate, scale, again = pl.pallas_call(
        column_kernel,
        in_specs=[pl.BlockSpec(memory_space=pltpu.VMEM)] * 2
        + [pl.BlockSpec(memory_space=pl.ANY)],
        out_specs=[pl.BlockSpec(memory_space=pltpu.VMEM)] * 2
        + [pl.BlockSpec(memory_space=pl.ANY)],
        out_shape=[jax.ShapeDtypeStruct(columns, jnp.float32)] * 2
        + [jax.ShapeDtypeStruct(again.shape, again.dtype)],
        input_output_aliases={2: 2},
        compiler_params=pltpu.CompilerParams(vmem_limit_bytes=4 * 2**20),
        name="head_columns",
        cost_estimate=long_hint,
    )(in_hbm(kerple_rate.reshape(1, -1)), in_hbm(kerple_scale.reshape(1, -1)), again)
    column = [packed] + [swap(packed, 2 * k) for k in range(1, line)]
    gathered = column + [swap(value, 1) for value in [again] + column[1:]]

    cache = in_vmem(jnp.swapaxes(latent_cache, 1, 2))
    all_rows = ctx * half
    message = (request_rows + STAT_ROWS, LANES)
    in_smem = pl.BlockSpec(memory_space=pltpu.SMEM)
    whole = pl.BlockSpec(memory_space=pltpu.VMEM)
    parts = []
    for b in range(requests):
        near, far = pl.pallas_call(
            functools.partial(attention_kernel, ctx=ctx, b=b),
            in_specs=[in_smem, in_smem] + [whole] * (ctx + 3),
            out_shape=[jax.ShapeDtypeStruct((line,) + message, jnp.bfloat16)] * 2,
            scratch_shapes=[
                pltpu.VMEM((all_rows, LAT + ROPE), jnp.bfloat16),
                pltpu.VMEM((all_rows, LAT), jnp.float32),
                pltpu.VMEM((all_rows, LANES), jnp.float32),
            ]
            + [pltpu.VMEM((all_rows, chunk), jnp.float32)] * 2
            + [pltpu.VMEM((all_rows, chunk), jnp.bfloat16)] * 2
            + [pltpu.VMEM((all_rows, LANES), jnp.float32)] * 2,
            compiler_params=pltpu.CompilerParams(vmem_limit_bytes=8 * 2**20),
            cost_estimate=hint,
            name="attention",
        )(in_hbm(page_order), in_hbm(lengths), *gathered, cache, inv_rate, scale)
        merged = pl.pallas_call(
            merge_kernel,
            out_shape=[jax.ShapeDtypeStruct(message, jnp.bfloat16) for _ in range(line)],
            compiler_params=pltpu.CompilerParams(vmem_limit_bytes=4 * 2**20),
            name="merge",
        )(near, swap(far, 1))
        parts.append(merged[0])
        parts += [swap(merged[k], 2 * k) for k in reversed(range(1, line))]

    tokens = requests * query_len
    weight = in_vmem(output_weight)
    small = pltpu.CompilerParams(vmem_limit_bytes=4 * 2**20)
    far, values = pl.pallas_call(
        output_kernel,
        out_shape=[
            jax.ShapeDtypeStruct((line, tokens, width), jnp.bfloat16),
            jax.ShapeDtypeStruct((8, output_weight.shape[0]), jnp.float32),
        ],
        scratch_shapes=[pltpu.VMEM((rows, LAT), jnp.bfloat16)],
        compiler_params=small,
        cost_estimate=hint,
        name="up_and_far_output",
    )(*parts, in_vmem(value_up), weight)
    near = pl.pallas_call(
        near_kernel,
        out_shape=jax.ShapeDtypeStruct((line, tokens, width), jnp.float32),
        compiler_params=small,
        cost_estimate=hint,
        name="near_output",
    )(values, weight)
    block = (tokens, width)
    kept, *sent = pl.pallas_call(
        add_kernel,
        out_shape=[jax.ShapeDtypeStruct(block, jnp.float32)]
        + [jax.ShapeDtypeStruct(block, jnp.bfloat16)] * 3,
        compiler_params=small,
        name="add_columns",
    )(near, swap(far, 2))
    return pl.pallas_call(
        sum_kernel,
        out_shape=jax.ShapeDtypeStruct((requests, query_len, width), jnp.bfloat16),
        compiler_params=small,
        name="sum_output",
    )(kept, *(swap(part, bits) for part, bits in reversed([*zip(sent, (1, 4, 5))])))


def plain_device(
    queries,
    key_absorb,
    latent_cache,
    page_order,
    lengths,
    kerple_scale,
    kerple_rate,
    value_up,
    output_weight,
    *,
    ctx,
):
    requests, query_len, heads, _ = queries.shape
    width = output_weight.shape[1] // ctx
    latent_query = jnp.einsum(
        "bqhn,hnc->bqhc", queries[..., :NOPE], key_absorb, preferred_element_type=jnp.float32
    ).astype(jnp.bfloat16)
    own_query = jnp.concatenate([latent_query, queries[..., NOPE:]], axis=-1)
    full_query = lax.all_gather(own_query, "ctx", axis=2, tiled=True)
    offsets = jnp.arange(PAGE, dtype=jnp.int32)
    key_pos = (page_order[:, :, None] * PAGE + offsets).reshape(requests, -1)
    query_pos = lengths[:, None] - query_len + jnp.arange(query_len, dtype=jnp.int32)
    distance = query_pos[:, :, None] - key_pos[:, None, :]
    visible = (distance >= 0)[:, :, None, :]
    spread = jnp.maximum(distance, 0).astype(jnp.float32)[:, :, None, :]
    log_bias = kerple_scale[:, None] * jnp.log(1.0 + kerple_rate[:, None] * spread)
    scores = jnp.einsum(
        "bqhc,btc->bqht", full_query, latent_cache, preferred_element_type=jnp.float32
    )
    scores = jnp.where(visible, scores * SOFTMAX_SCALE - log_bias, LOWEST)
    row_max = jnp.max(scores, axis=-1)
    weights = jnp.where(visible, jnp.exp(scores - row_max[..., None]), 0.0)
    summed = jnp.einsum(
        "bqht,btc->bqhc",
        weights.astype(jnp.bfloat16),
        latent_cache[..., :LAT],
        preferred_element_type=jnp.float32,
    )
    factor = jnp.exp(row_max - lax.pmax(row_max, "ctx"))
    shared_total = lax.psum_scatter(
        jnp.sum(weights, axis=-1) * factor, "ctx", scatter_dimension=2, tiled=True
    )
    shared_sum = lax.psum_scatter(
        summed * factor[..., None], "ctx", scatter_dimension=2, tiled=True
    )
    attn_latent = (shared_sum / shared_total[..., None]).astype(jnp.bfloat16)
    up_values = jnp.einsum(
        "bqhc,hcv->bqhv", attn_latent, value_up, preferred_element_type=jnp.float32
    ).astype(jnp.bfloat16)
    partial_out = jnp.dot(
        up_values.reshape(requests * query_len, -1),
        output_weight,
        preferred_element_type=jnp.float32,
    )
    summed_out = lax.psum_scatter(partial_out, "ctx", scatter_dimension=1, tiled=True)
    return summed_out.astype(jnp.bfloat16).reshape(requests, query_len, width)


def solution(mesh):
    ctx = mesh.shape["ctx"]
    in_specs = (
        P("rep", None, "ctx", None),
        P("ctx", None, None),
        P("rep", "ctx", None),
        P("rep", "ctx"),
        P("rep"),
        P(),
        P(),
        P("ctx", None, None),
        P("ctx", None),
    )
    out_specs = P("rep", None, "ctx")

    def device_program(*args):
        heads = args[0].shape[2]
        width = args[-1].shape[1] // ctx
        tiled = ctx == 8 and heads % 16 == 0 and width % LANES == 0
        return (per_device if tiled else plain_device)(*args, ctx=ctx)

    return jax.shard_map(
        device_program, mesh=mesh, in_specs=in_specs, out_specs=out_specs, check_vma=False
    )
```

```python
import functools

import jax
import jax.numpy as jnp
from jax import lax
from jax.experimental import pallas as pl
from jax.experimental.pallas import tpu as pltpu
from jax.sharding import PartitionSpec as P

NOPE = 128
ROPE = 64
LAT = 512
PAGE = 128
LANES = 128
LAT_TILES = LAT // LANES
LOG2E = 1.4426950408889634
SOFTMAX_SCALE = (NOPE + ROPE) ** (-0.5)
LOWEST = -1e30
STAT_ROWS = 16


def head_of_row(shape, heads):
    return lax.rem(lax.broadcasted_iota(jnp.int32, shape, 0), heads)


def query_kernel(queries_hbm, absorb_hbm, out_ref, again_ref, queries_ref, absorb_ref, sems):
    rows = queries_ref.shape[0]
    heads = absorb_ref.shape[0]
    half = rows // 2
    pieces = sems.shape[0] - 1
    group = heads // pieces
    copies = [pltpu.make_async_copy(queries_hbm, queries_ref, sems.at[pieces])] + [
        pltpu.make_async_copy(
            absorb_hbm.at[pl.ds(i * group, group)],
            absorb_ref.at[pl.ds(i * group, group)],
            sems.at[i],
        )
        for i in range(pieces)
    ]
    for copy in copies:
        copy.start()
    copies[0].wait()
    nope = queries_ref[:, :NOPE]
    owner = head_of_row((rows, NOPE), heads)
    latent = jnp.zeros((rows, LAT), jnp.float32)
    for i in range(pieces):
        spread = jnp.concatenate(
            [
                jnp.where(owner == h, nope, jnp.zeros_like(nope))
                for h in range(i * group, (i + 1) * group)
            ],
            axis=1,
        )
        copies[i + 1].wait()
        latent += jnp.dot(
            spread,
            absorb_ref[i * group : (i + 1) * group].reshape(group * NOPE, LAT),
            preferred_element_type=jnp.float32,
        )
    latent = latent.astype(jnp.bfloat16)
    rope = queries_ref[:, NOPE:]
    rope = jnp.concatenate([rope[:half], rope[half:]], axis=1)
    for b in range(2):
        for j in range(LAT_TILES):
            start = (b * LAT_TILES + j) * half
            out_ref[start : start + half, :] = latent[
                b * half : (b + 1) * half, j * LANES : (j + 1) * LANES
            ]
    out_ref[2 * LAT_TILES * half :, :] = rope
    again_ref[...] = out_ref[...]


def column_kernel(rate_ref, scale_ref, through_ref, inv_rate_ref, scales_ref, passed_ref):
    del through_ref, passed_ref
    ctx, heads, _ = inv_rate_ref.shape
    line = ctx // 2
    me = lax.axis_index("ctx")
    for source, target in ((1.0 / rate_ref[...], inv_rate_ref), (scale_ref[...], scales_ref)):
        size = source.shape[1]
        same = lax.broadcasted_iota(jnp.int32, (size, size), 0) == lax.broadcasted_iota(
            jnp.int32, (size, size), 1
        )
        column = jnp.sum(jnp.where(same, source, 0.0), axis=1, keepdims=True)
        column = jnp.broadcast_to(column, (size, LANES)).reshape(ctx, heads, LANES)
        for k in range(ctx):
            owner = me ^ (2 * (k % line) + k // line)
            picked = jnp.zeros((heads, LANES), jnp.float32)
            for device in range(ctx):
                picked = jnp.where(owner == device, column[device], picked)
            target[k] = picked


def attention_kernel(pages_ref, lengths_ref, *refs, ctx, b):
    query_refs, refs = refs[:ctx], refs[ctx:]
    cache_ref, inv_rate, scale, near_ref, far_ref, query, acc, total, *buffers = refs
    scores_of, weights_of, factor_of = buffers[:2], buffers[2:4], buffers[4:]
    rows, chunk = scores_of[0].shape
    half = rows // ctx
    heads = half // 2
    line = ctx // 2
    steps = cache_ref.shape[2] // chunk
    pair_width = 2 * PAGE
    pairs = chunk // pair_width
    request_rows = LAT_TILES * half
    start = b * request_rows

    for k, block in enumerate(query_refs):
        own = slice(k * half, (k + 1) * half)
        for j in range(LAT_TILES):
            query[own, j * LANES : (j + 1) * LANES] = block[
                start + j * half : start + (j + 1) * half, :
            ]
        query[own, LAT:] = block[2 * request_rows :, b * ROPE : (b + 1) * ROPE]

    lane = lax.broadcasted_iota(jnp.int32, (heads, LANES), 1)
    first_pos = lengths_ref[b] - 2

    def raw_scores(at):
        return jnp.dot(
            query[...],
            cache_ref[b, :, at * pair_width : (at + 1) * pair_width],
            preferred_element_type=jnp.float32,
        )

    def add_products(step):
        weights, factor = weights_of[step % 2], factor_of[step % 2]
        for columns in (slice(0, LAT // 2), slice(LAT // 2, LAT)):
            new = lax.dot_general(
                weights[...],
                cache_ref[b, columns, step * chunk : (step + 1) * chunk],
                (((1,), (1,)), ((), ())),
                preferred_element_type=jnp.float32,
            )
            for j in range(columns.start, columns.stop, LANES):
                part = new[:, j - columns.start : j - columns.start + LANES]
                at = slice(j, j + LANES)
                acc[:, at] = acc[:, at] * factor[...] + part if step else part

    top = jnp.full((rows, LANES), LOWEST, jnp.float32)
    ahead = raw_scores(0)
    for step in range(steps):
        scores, weights = scores_of[step % 2], weights_of[step % 2]
        tops = [None, None]
        for pair in range(pairs):
            raw = ahead
            at = step * pairs + pair
            if at + 1 < steps * pairs:
                ahead = raw_scores(at + 1)
            for side in range(2):
                page = pair * 2 + side
                columns = slice(page * PAGE, (page + 1) * PAGE)
                part = raw[:, side * PAGE : (side + 1) * PAGE].reshape(ctx, 2, heads, PAGE)
                base = first_pos - pages_ref[b, step * (chunk // PAGE) + page] * PAGE
                values = []
                for q in range(2):
                    distance = base + q - lane
                    spread = jnp.where(distance >= 0, distance.astype(jnp.float32), jnp.inf)
                    logs = jnp.log2(spread[None] + inv_rate[...])
                    value = part[:, q] * (SOFTMAX_SCALE * LOG2E) - scale[...] * logs
                    tops[q] = value if tops[q] is None else jnp.maximum(tops[q], value)
                    values.append(value)
                scores[:, columns] = jnp.stack(values, axis=1).reshape(rows, PAGE)
        lane_top = jnp.stack(tops, axis=1).reshape(rows, LANES)
        before = top
        top = jnp.maximum(before, jnp.max(lane_top, axis=1, keepdims=True))
        factor = jnp.exp2(before - top)
        factor_of[step % 2][...] = factor
        if step:
            add_products(step - 1)
        lane_total = total[...] * factor if step else jnp.zeros((rows, LANES), jnp.float32)
        for page in range(chunk // PAGE):
            columns = slice(page * PAGE, (page + 1) * PAGE)
            value = jnp.exp2(scores[:, columns] - top)
            lane_total += value
            weights[:, columns] = value.astype(jnp.bfloat16)
        total[...] = lane_total
    add_products(steps - 1)

    row_total = jnp.sum(total[...], axis=1, keepdims=True)
    row_total = jnp.broadcast_to(row_total, (rows, LANES))
    seen = row_total > 0.0
    safe = jnp.where(seen, row_total, 1.0)
    share = 1.0 / safe
    for j in range(LAT_TILES):
        columns = slice(j * LANES, (j + 1) * LANES)
        part = (acc[:, columns] * share).astype(jnp.bfloat16).reshape(ctx, half, LANES)
        near_ref[:, j * half : (j + 1) * half, :] = part[:line]
        far_ref[:, j * half : (j + 1) * half, :] = part[line:]
    log_total = jnp.where(seen, top + jnp.log2(safe), LOWEST).reshape(ctx, half, LANES)
    across = jnp.sum(jnp.where(diagonal(half), log_total, 0.0), axis=1, keepdims=True)
    packed = three_parts(across).astype(jnp.bfloat16)
    near_ref[:, request_rows:, :] = packed[:line]
    far_ref[:, request_rows:, :] = packed[line:]


def diagonal(half):
    return lax.broadcasted_iota(jnp.int32, (half, LANES), 0) == lax.broadcasted_iota(
        jnp.int32, (half, LANES), 1
    )


def three_parts(value):
    high = value.astype(jnp.bfloat16).astype(jnp.float32)
    middle = (value - high).astype(jnp.bfloat16).astype(jnp.float32)
    low = value - high - middle
    row = lax.broadcasted_iota(jnp.int32, (value.shape[0], STAT_ROWS, LANES), 1)
    return jnp.where(
        row == 0, high, jnp.where(row == 1, middle, jnp.where(row == 2, low, 0.0))
    )


def logs_of(stats):
    return jnp.sum(stats.astype(jnp.float32), axis=1, keepdims=True)


def as_column(across, half):
    return jnp.sum(jnp.where(diagonal(half), across, 0.0), axis=-1, keepdims=True)


def merge_kernel(own_ref, other_ref, *out_refs):
    request_rows = own_ref.shape[1] - STAT_ROWS
    half = request_rows // LAT_TILES
    own_log = logs_of(own_ref[:, request_rows:, :])
    other_log = logs_of(other_ref[:, request_rows:, :])
    high = jnp.maximum(own_log, other_log)
    own_factor = jnp.exp2(own_log - high)
    other_factor = jnp.exp2(other_log - high)
    both = own_factor + other_factor
    stats = three_parts(high + jnp.log2(both)).astype(jnp.bfloat16)
    own_factor = as_column(own_factor / both, half)
    other_factor = as_column(other_factor / both, half)
    for j in range(LAT_TILES):
        at = slice(j * half, (j + 1) * half)
        merged = (
            own_ref[:, at, :].astype(jnp.float32) * own_factor
            + other_ref[:, at, :].astype(jnp.float32) * other_factor
        ).astype(jnp.bfloat16)
        for k, out_ref in enumerate(out_refs):
            out_ref[at, :] = merged[k]
    for k, out_ref in enumerate(out_refs):
        out_ref[request_rows:, :] = stats[k]


def output_kernel(*refs):
    *part_refs, up_ref, weight_ref, out_ref, values, attn = refs
    heads = up_ref.shape[0]
    half = 2 * heads
    rows = 2 * half
    request_rows = LAT_TILES * half
    for b in range(2):
        parts = part_refs[b * len(part_refs) // 2 : (b + 1) * len(part_refs) // 2]
        logs = logs_of(jnp.stack([part[request_rows:, :] for part in parts]))
        factor = jnp.exp2(logs - jnp.max(logs, axis=0, keepdims=True))
        factor = as_column(factor / jnp.sum(factor, axis=0, keepdims=True), half)
        for j in range(LAT_TILES):
            at = slice(j * half, (j + 1) * half)
            attn[b * half : (b + 1) * half, j * LANES : (j + 1) * LANES] = sum(
                part[at, :].astype(jnp.float32) * factor[k] for k, part in enumerate(parts)
            ).astype(jnp.bfloat16)
    latent = attn[...]
    owner = head_of_row(latent.shape, heads)
    up = jnp.zeros((rows, up_ref.shape[2]), jnp.float32)
    for h in range(heads):
        own = jnp.where(owner == h, latent, jnp.zeros_like(latent))
        up += jnp.dot(own, up_ref[h], preferred_element_type=jnp.float32)
    up = up.astype(jnp.bfloat16)
    owner = head_of_row(up.shape, heads)
    spread = jnp.concatenate(
        [jnp.where(owner == h, up, jnp.zeros_like(up)) for h in range(heads)], axis=1
    )
    token = lax.broadcasted_iota(jnp.int32, (8, rows), 0)
    group = lax.broadcasted_iota(jnp.int32, (8, rows), 1) // heads
    pick = jnp.where(token == group, 1.0, 0.0).astype(jnp.bfloat16)
    values[...] = jnp.dot(pick, spread, preferred_element_type=jnp.float32)
    project(values, weight_ref, out_ref, True)


def project(values, weight_ref, out_ref, far):
    blocks, tokens, width = out_ref.shape
    bit = lax.axis_index("ctx") // blocks
    first = (1 - bit if far else bit) * (blocks * width)

    @pl.loop(0, blocks // 2)
    def _(k):
        result = jnp.dot(
            values[...].astype(jnp.bfloat16),
            weight_ref[:, pl.ds(pl.multiple_of(first + k * (2 * width), LANES), 2 * width)],
            preferred_element_type=jnp.float32,
        )
        out_ref[2 * k] = result[:tokens, :width].astype(out_ref.dtype)
        out_ref[2 * k + 1] = result[:tokens, width:].astype(out_ref.dtype)


def near_kernel(values, weight_ref, out_ref):
    project(values, weight_ref, out_ref, False)


def add_kernel(own_ref, other_ref, kept_ref, *sent_refs):
    own = lax.rem(lax.axis_index("ctx"), own_ref.shape[0])
    for k, out_ref in enumerate((kept_ref,) + sent_refs):
        block = own_ref[own ^ k] + other_ref[own ^ k].astype(jnp.float32)
        out_ref[...] = block.astype(out_ref.dtype)


def sum_kernel(own_ref, *refs):
    *other_refs, out_ref = refs
    result = own_ref[...]
    for other in other_refs:
        result += other[...].astype(jnp.float32)
    requests, tokens, _ = out_ref.shape
    for b in range(requests):
        out_ref[b] = result[b * tokens : (b + 1) * tokens].astype(out_ref.dtype)


def per_device(
    queries,
    key_absorb,
    latent_cache,
    page_order,
    lengths,
    kerple_scale,
    kerple_rate,
    value_up,
    output_weight,
    *,
    ctx,
):
    requests, query_len, heads, query_width = queries.shape
    keys_dev = latent_cache.shape[1]
    half = query_len * heads
    rows = requests * half
    request_rows = LAT_TILES * half
    width = output_weight.shape[1] // ctx
    chunk = 1024

    hint = pl.CostEstimate(flops=20 * 10**9, bytes_accessed=2**20, transcendentals=0)
    long_hint = pl.CostEstimate(flops=100 * 10**9, bytes_accessed=2**20, transcendentals=0)
    in_hbm = lambda value: pltpu.with_memory_space_constraint(value, pltpu.HBM)
    in_vmem = lambda value: pltpu.with_memory_space_constraint(value, pltpu.VMEM)
    line = ctx // 2
    swap = lambda value, bits: lax.ppermute(value, "ctx", [(i, i ^ bits) for i in range(ctx)])
    packed, again = pl.pallas_call(
        query_kernel,
        in_specs=[pl.BlockSpec(memory_space=pl.ANY)] * 2,
        out_shape=[jax.ShapeDtypeStruct((2 * request_rows + half, LANES), jnp.bfloat16)] * 2,
        scratch_shapes=[
            pltpu.VMEM((rows, query_width), jnp.bfloat16),
            pltpu.VMEM(key_absorb.shape, jnp.bfloat16),
            pltpu.SemaphoreType.DMA((5,)),
        ],
        compiler_params=pltpu.CompilerParams(vmem_limit_bytes=8 * 2**20),
        name="latent_query",
    )(in_hbm(queries.reshape(rows, query_width)), in_hbm(key_absorb))
    columns = (ctx, heads, LANES)
    inv_rate, scale, again = pl.pallas_call(
        column_kernel,
        in_specs=[pl.BlockSpec(memory_space=pltpu.VMEM)] * 2
        + [pl.BlockSpec(memory_space=pl.ANY)],
        out_specs=[pl.BlockSpec(memory_space=pltpu.VMEM)] * 2
        + [pl.BlockSpec(memory_space=pl.ANY)],
        out_shape=[jax.ShapeDtypeStruct(columns, jnp.float32)] * 2
        + [jax.ShapeDtypeStruct(again.shape, again.dtype)],
        input_output_aliases={2: 2},
        compiler_params=pltpu.CompilerParams(vmem_limit_bytes=4 * 2**20),
        name="head_columns",
        cost_estimate=long_hint,
    )(in_hbm(kerple_rate.reshape(1, -1)), in_hbm(kerple_scale.reshape(1, -1)), again)
    column = [packed] + [swap(packed, 2 * k) for k in range(1, line)]
    gathered = column + [swap(value, 1) for value in [again] + column[1:]]

    cache = in_vmem(jnp.swapaxes(latent_cache, 1, 2))
    all_rows = ctx * half
    message = (request_rows + STAT_ROWS, LANES)
    in_smem = pl.BlockSpec(memory_space=pltpu.SMEM)
    whole = pl.BlockSpec(memory_space=pltpu.VMEM)
    parts = []
    for b in range(requests):
        near, far = pl.pallas_call(
            functools.partial(attention_kernel, ctx=ctx, b=b),
            in_specs=[in_smem, in_smem] + [whole] * (ctx + 3),
            out_shape=[jax.ShapeDtypeStruct((line,) + message, jnp.bfloat16)] * 2,
            scratch_shapes=[
                pltpu.VMEM((all_rows, LAT + ROPE), jnp.bfloat16),
                pltpu.VMEM((all_rows, LAT), jnp.float32),
                pltpu.VMEM((all_rows, LANES), jnp.float32),
            ]
            + [pltpu.VMEM((all_rows, chunk), jnp.float32)] * 2
            + [pltpu.VMEM((all_rows, chunk), jnp.bfloat16)] * 2
            + [pltpu.VMEM((all_rows, LANES), jnp.float32)] * 2,
            compiler_params=pltpu.CompilerParams(vmem_limit_bytes=8 * 2**20),
            cost_estimate=hint,
            name="attention",
        )(in_hbm(page_order), in_hbm(lengths), *gathered, cache, inv_rate, scale)
        merged = pl.pallas_call(
            merge_kernel,
            out_shape=[jax.ShapeDtypeStruct(message, jnp.bfloat16) for _ in range(line)],
            compiler_params=pltpu.CompilerParams(vmem_limit_bytes=4 * 2**20),
            name="merge",
        )(near, swap(far, 1))
        parts.append(merged[0])
        parts += [swap(merged[k], 2 * k) for k in reversed(range(1, line))]

    tokens = requests * query_len
    weight = in_vmem(output_weight)
    small = pltpu.CompilerParams(vmem_limit_bytes=4 * 2**20)
    far, values = pl.pallas_call(
        output_kernel,
        out_shape=[
            jax.ShapeDtypeStruct((line, tokens, width), jnp.bfloat16),
            jax.ShapeDtypeStruct((8, output_weight.shape[0]), jnp.float32),
        ],
        scratch_shapes=[pltpu.VMEM((rows, LAT), jnp.bfloat16)],
        compiler_params=small,
        cost_estimate=hint,
        name="up_and_far_output",
    )(*parts, in_vmem(value_up), weight)
    near = pl.pallas_call(
        near_kernel,
        out_shape=jax.ShapeDtypeStruct((line, tokens, width), jnp.float32),
        compiler_params=small,
        cost_estimate=hint,
        name="near_output",
    )(values, weight)
    block = (tokens, width)
    kept, *sent = pl.pallas_call(
        add_kernel,
        out_shape=[jax.ShapeDtypeStruct(block, jnp.float32)]
        + [jax.ShapeDtypeStruct(block, jnp.bfloat16)] * 3,
        compiler_params=small,
        name="add_columns",
    )(near, swap(far, 4))
    return pl.pallas_call(
        sum_kernel,
        out_shape=jax.ShapeDtypeStruct((requests, query_len, width), jnp.bfloat16),
        compiler_params=small,
        name="sum_output",
    )(kept, *(swap(part, bits) for part, bits in reversed([*zip(sent, (1, 2, 3))])))


def plain_device(
    queries,
    key_absorb,
    latent_cache,
    page_order,
    lengths,
    kerple_scale,
    kerple_rate,
    value_up,
    output_weight,
    *,
    ctx,
):
    requests, query_len, heads, _ = queries.shape
    width = output_weight.shape[1] // ctx
    latent_query = jnp.einsum(
        "bqhn,hnc->bqhc", queries[..., :NOPE], key_absorb, preferred_element_type=jnp.float32
    ).astype(jnp.bfloat16)
    own_query = jnp.concatenate([latent_query, queries[..., NOPE:]], axis=-1)
    full_query = lax.all_gather(own_query, "ctx", axis=2, tiled=True)
    offsets = jnp.arange(PAGE, dtype=jnp.int32)
    key_pos = (page_order[:, :, None] * PAGE + offsets).reshape(requests, -1)
    query_pos = lengths[:, None] - query_len + jnp.arange(query_len, dtype=jnp.int32)
    distance = query_pos[:, :, None] - key_pos[:, None, :]
    visible = (distance >= 0)[:, :, None, :]
    spread = jnp.maximum(distance, 0).astype(jnp.float32)[:, :, None, :]
    log_bias = kerple_scale[:, None] * jnp.log(1.0 + kerple_rate[:, None] * spread)
    scores = jnp.einsum(
        "bqhc,btc->bqht", full_query, latent_cache, preferred_element_type=jnp.float32
    )
    scores = jnp.where(visible, scores * SOFTMAX_SCALE - log_bias, LOWEST)
    row_max = jnp.max(scores, axis=-1)
    weights = jnp.where(visible, jnp.exp(scores - row_max[..., None]), 0.0)
    summed = jnp.einsum(
        "bqht,btc->bqhc",
        weights.astype(jnp.bfloat16),
        latent_cache[..., :LAT],
        preferred_element_type=jnp.float32,
    )
    factor = jnp.exp(row_max - lax.pmax(row_max, "ctx"))
    shared_total = lax.psum_scatter(
        jnp.sum(weights, axis=-1) * factor, "ctx", scatter_dimension=2, tiled=True
    )
    shared_sum = lax.psum_scatter(
        summed * factor[..., None], "ctx", scatter_dimension=2, tiled=True
    )
    attn_latent = (shared_sum / shared_total[..., None]).astype(jnp.bfloat16)
    up_values = jnp.einsum(
        "bqhc,hcv->bqhv", attn_latent, value_up, preferred_element_type=jnp.float32
    ).astype(jnp.bfloat16)
    partial_out = jnp.dot(
        up_values.reshape(requests * query_len, -1),
        output_weight,
        preferred_element_type=jnp.float32,
    )
    summed_out = lax.psum_scatter(partial_out, "ctx", scatter_dimension=1, tiled=True)
    return summed_out.astype(jnp.bfloat16).reshape(requests, query_len, width)


def solution(mesh):
    ctx = mesh.shape["ctx"]
    in_specs = (
        P("rep", None, "ctx", None),
        P("ctx", None, None),
        P("rep", "ctx", None),
        P("rep", "ctx"),
        P("rep"),
        P(),
        P(),
        P("ctx", None, None),
        P("ctx", None),
    )
    out_specs = P("rep", None, "ctx")

    def device_program(*args):
        heads = args[0].shape[2]
        width = args[-1].shape[1] // ctx
        tiled = ctx == 8 and heads % 16 == 0 and width % LANES == 0
        return (per_device if tiled else plain_device)(*args, ctx=ctx)

    return jax.shard_map(
        device_program, mesh=mesh, in_specs=in_specs, out_specs=out_specs, check_vma=False
    )
```

```python
import functools

import jax
import jax.numpy as jnp
from jax import lax
from jax.experimental import pallas as pl
from jax.experimental.pallas import tpu as pltpu
from jax.sharding import PartitionSpec as P

NOPE = 128
ROPE = 64
LAT = 512
PAGE = 128
LANES = 128
LAT_TILES = LAT // LANES
LOG2E = 1.4426950408889634
SOFTMAX_SCALE = (NOPE + ROPE) ** (-0.5)
LOWEST = -1e30
STAT_ROWS = 16


def head_of_row(shape, heads):
    return lax.rem(lax.broadcasted_iota(jnp.int32, shape, 0), heads)


def query_kernel(queries_hbm, absorb_hbm, out_ref, again_ref, queries_ref, absorb_ref, sems):
    rows = queries_ref.shape[0]
    heads = absorb_ref.shape[0]
    half = rows // 2
    pieces = sems.shape[0] - 1
    group = heads // pieces
    copies = [pltpu.make_async_copy(queries_hbm, queries_ref, sems.at[pieces])] + [
        pltpu.make_async_copy(
            absorb_hbm.at[pl.ds(i * group, group)],
            absorb_ref.at[pl.ds(i * group, group)],
            sems.at[i],
        )
        for i in range(pieces)
    ]
    for copy in copies:
        copy.start()
    copies[0].wait()
    nope = queries_ref[:, :NOPE]
    owner = head_of_row((rows, NOPE), heads)
    latent = jnp.zeros((rows, LAT), jnp.float32)
    for i in range(pieces):
        spread = jnp.concatenate(
            [
                jnp.where(owner == h, nope, jnp.zeros_like(nope))
                for h in range(i * group, (i + 1) * group)
            ],
            axis=1,
        )
        copies[i + 1].wait()
        latent += jnp.dot(
            spread,
            absorb_ref[i * group : (i + 1) * group].reshape(group * NOPE, LAT),
            preferred_element_type=jnp.float32,
        )
    latent = latent.astype(jnp.bfloat16)
    rope = queries_ref[:, NOPE:]
    rope = jnp.concatenate([rope[:half], rope[half:]], axis=1)
    for b in range(2):
        for j in range(LAT_TILES):
            start = (b * LAT_TILES + j) * half
            out_ref[start : start + half, :] = latent[
                b * half : (b + 1) * half, j * LANES : (j + 1) * LANES
            ]
    out_ref[2 * LAT_TILES * half :, :] = rope
    again_ref[...] = out_ref[...]


def column_kernel(rate_ref, scale_ref, through_ref, inv_rate_ref, scales_ref, passed_ref):
    del through_ref, passed_ref
    ctx, heads, _ = inv_rate_ref.shape
    line = ctx // 2
    me = lax.axis_index("ctx")
    for source, target in ((1.0 / rate_ref[...], inv_rate_ref), (scale_ref[...], scales_ref)):
        size = source.shape[1]
        same = lax.broadcasted_iota(jnp.int32, (size, size), 0) == lax.broadcasted_iota(
            jnp.int32, (size, size), 1
        )
        column = jnp.sum(jnp.where(same, source, 0.0), axis=1, keepdims=True)
        column = jnp.broadcast_to(column, (size, LANES)).reshape(ctx, heads, LANES)
        for k in range(ctx):
            owner = me ^ (2 * (k % line) + k // line)
            picked = jnp.zeros((heads, LANES), jnp.float32)
            for device in range(ctx):
                picked = jnp.where(owner == device, column[device], picked)
            target[k] = picked


def attention_kernel(pages_ref, lengths_ref, *refs, ctx, b):
    query_refs, refs = refs[:ctx], refs[ctx:]
    cache_ref, inv_rate, scale, near_ref, far_ref, query, acc, total, *buffers = refs
    scores_of, weights_of, factor_of = buffers[:2], buffers[2:4], buffers[4:]
    rows, chunk = scores_of[0].shape
    half = rows // ctx
    heads = half // 2
    line = ctx // 2
    steps = cache_ref.shape[2] // chunk
    pair_width = 2 * PAGE
    pairs = chunk // pair_width
    request_rows = LAT_TILES * half
    start = b * request_rows

    for k, block in enumerate(query_refs):
        own = slice(k * half, (k + 1) * half)
        for j in range(LAT_TILES):
            query[own, j * LANES : (j + 1) * LANES] = block[
                start + j * half : start + (j + 1) * half, :
            ]
        query[own, LAT:] = block[2 * request_rows :, b * ROPE : (b + 1) * ROPE]

    lane = lax.broadcasted_iota(jnp.int32, (heads, LANES), 1)
    first_pos = lengths_ref[b] - 2

    def raw_scores(at):
        return jnp.dot(
            query[...],
            cache_ref[b, :, at * pair_width : (at + 1) * pair_width],
            preferred_element_type=jnp.float32,
        )

    def add_products(step):
        weights, factor = weights_of[step % 2], factor_of[step % 2]
        for columns in (slice(0, LAT // 2), slice(LAT // 2, LAT)):
            new = lax.dot_general(
                weights[...],
                cache_ref[b, columns, step * chunk : (step + 1) * chunk],
                (((1,), (1,)), ((), ())),
                preferred_element_type=jnp.float32,
            )
            for j in range(columns.start, columns.stop, LANES):
                part = new[:, j - columns.start : j - columns.start + LANES]
                at = slice(j, j + LANES)
                acc[:, at] = acc[:, at] * factor[...] + part if step else part

    top = jnp.full((rows, LANES), LOWEST, jnp.float32)
    ahead = raw_scores(0)
    for step in range(steps):
        scores, weights = scores_of[step % 2], weights_of[step % 2]
        tops = [None, None]
        for pair in range(pairs):
            raw = ahead
            at = step * pairs + pair
            if at + 1 < steps * pairs:
                ahead = raw_scores(at + 1)
            for side in range(2):
                page = pair * 2 + side
                columns = slice(page * PAGE, (page + 1) * PAGE)
                part = raw[:, side * PAGE : (side + 1) * PAGE].reshape(ctx, 2, heads, PAGE)
                base = first_pos - pages_ref[b, step * (chunk // PAGE) + page] * PAGE
                values = []
                for q in range(2):
                    distance = base + q - lane
                    spread = jnp.where(distance >= 0, distance.astype(jnp.float32), jnp.inf)
                    logs = jnp.log2(spread[None] + inv_rate[...])
                    value = part[:, q] * (SOFTMAX_SCALE * LOG2E) - scale[...] * logs
                    tops[q] = value if tops[q] is None else jnp.maximum(tops[q], value)
                    values.append(value)
                scores[:, columns] = jnp.stack(values, axis=1).reshape(rows, PAGE)
        lane_top = jnp.stack(tops, axis=1).reshape(rows, LANES)
        before = top
        top = jnp.maximum(before, jnp.max(lane_top, axis=1, keepdims=True))
        factor = jnp.exp2(before - top)
        factor_of[step % 2][...] = factor
        if step:
            add_products(step - 1)
        lane_total = total[...] * factor if step else jnp.zeros((rows, LANES), jnp.float32)
        for page in range(chunk // PAGE):
            columns = slice(page * PAGE, (page + 1) * PAGE)
            value = jnp.exp2(scores[:, columns] - top)
            lane_total += value
            weights[:, columns] = value.astype(jnp.bfloat16)
        total[...] = lane_total
    add_products(steps - 1)

    row_total = jnp.sum(total[...], axis=1, keepdims=True)
    row_total = jnp.broadcast_to(row_total, (rows, LANES))
    seen = row_total > 0.0
    safe = jnp.where(seen, row_total, 1.0)
    share = 1.0 / safe
    for j in range(LAT_TILES):
        columns = slice(j * LANES, (j + 1) * LANES)
        part = (acc[:, columns] * share).astype(jnp.bfloat16).reshape(ctx, half, LANES)
        near_ref[:, j * half : (j + 1) * half, :] = part[:line]
        far_ref[:, j * half : (j + 1) * half, :] = part[line:]
    log_total = jnp.where(seen, top + jnp.log2(safe), LOWEST).reshape(ctx, half, LANES)
    across = jnp.sum(jnp.where(diagonal(half), log_total, 0.0), axis=1, keepdims=True)
    packed = three_parts(across).astype(jnp.bfloat16)
    near_ref[:, request_rows:, :] = packed[:line]
    far_ref[:, request_rows:, :] = packed[line:]


def diagonal(half):
    return lax.broadcasted_iota(jnp.int32, (half, LANES), 0) == lax.broadcasted_iota(
        jnp.int32, (half, LANES), 1
    )


def three_parts(value):
    high = value.astype(jnp.bfloat16).astype(jnp.float32)
    middle = (value - high).astype(jnp.bfloat16).astype(jnp.float32)
    low = value - high - middle
    row = lax.broadcasted_iota(jnp.int32, (value.shape[0], STAT_ROWS, LANES), 1)
    return jnp.where(
        row == 0, high, jnp.where(row == 1, middle, jnp.where(row == 2, low, 0.0))
    )


def logs_of(stats):
    return jnp.sum(stats.astype(jnp.float32), axis=1, keepdims=True)


def as_column(across, half):
    return jnp.sum(jnp.where(diagonal(half), across, 0.0), axis=-1, keepdims=True)


def merge_kernel(own_ref, other_ref, *out_refs):
    request_rows = own_ref.shape[1] - STAT_ROWS
    half = request_rows // LAT_TILES
    own_log = logs_of(own_ref[:, request_rows:, :])
    other_log = logs_of(other_ref[:, request_rows:, :])
    high = jnp.maximum(own_log, other_log)
    own_factor = jnp.exp2(own_log - high)
    other_factor = jnp.exp2(other_log - high)
    both = own_factor + other_factor
    stats = three_parts(high + jnp.log2(both)).astype(jnp.bfloat16)
    own_factor = as_column(own_factor / both, half)
    other_factor = as_column(other_factor / both, half)
    for j in range(LAT_TILES):
        at = slice(j * half, (j + 1) * half)
        merged = (
            own_ref[:, at, :].astype(jnp.float32) * own_factor
            + other_ref[:, at, :].astype(jnp.float32) * other_factor
        ).astype(jnp.bfloat16)
        for k, out_ref in enumerate(out_refs):
            out_ref[at, :] = merged[k]
    for k, out_ref in enumerate(out_refs):
        out_ref[request_rows:, :] = stats[k]


def output_kernel(*refs):
    *part_refs, up_ref, weight_ref, out_ref, values, attn = refs
    heads = up_ref.shape[0]
    half = 2 * heads
    rows = 2 * half
    request_rows = LAT_TILES * half
    for b in range(2):
        parts = part_refs[b * len(part_refs) // 2 : (b + 1) * len(part_refs) // 2]
        logs = logs_of(jnp.stack([part[request_rows:, :] for part in parts]))
        factor = jnp.exp2(logs - jnp.max(logs, axis=0, keepdims=True))
        factor = as_column(factor / jnp.sum(factor, axis=0, keepdims=True), half)
        for j in range(LAT_TILES):
            at = slice(j * half, (j + 1) * half)
            attn[b * half : (b + 1) * half, j * LANES : (j + 1) * LANES] = sum(
                part[at, :].astype(jnp.float32) * factor[k] for k, part in enumerate(parts)
            ).astype(jnp.bfloat16)
    latent = attn[...]
    owner = head_of_row(latent.shape, heads)
    up = jnp.zeros((rows, up_ref.shape[2]), jnp.float32)
    for h in range(heads):
        own = jnp.where(owner == h, latent, jnp.zeros_like(latent))
        up += jnp.dot(own, up_ref[h], preferred_element_type=jnp.float32)
    up = up.astype(jnp.bfloat16)
    owner = head_of_row(up.shape, heads)
    spread = jnp.concatenate(
        [jnp.where(owner == h, up, jnp.zeros_like(up)) for h in range(heads)], axis=1
    )
    token = lax.broadcasted_iota(jnp.int32, (8, rows), 0)
    group = lax.broadcasted_iota(jnp.int32, (8, rows), 1) // heads
    pick = jnp.where(token == group, 1.0, 0.0).astype(jnp.bfloat16)
    values[...] = jnp.dot(pick, spread, preferred_element_type=jnp.float32)
    project(values, weight_ref, out_ref, True)


def project(values, weight_ref, out_ref, far):
    blocks, tokens, width = out_ref.shape
    bit = lax.rem(lax.axis_index("ctx") // 2, 2)
    first = (1 - bit if far else bit) * (2 * width)

    @pl.loop(0, blocks // 2)
    def _(k):
        result = jnp.dot(
            values[...].astype(jnp.bfloat16),
            weight_ref[:, pl.ds(pl.multiple_of(first + k * (4 * width), LANES), 2 * width)],
            preferred_element_type=jnp.float32,
        )
        out_ref[2 * k] = result[:tokens, :width].astype(out_ref.dtype)
        out_ref[2 * k + 1] = result[:tokens, width:].astype(out_ref.dtype)


def near_kernel(values, weight_ref, out_ref):
    project(values, weight_ref, out_ref, False)


def add_kernel(own_ref, other_ref, kept_ref, *sent_refs):
    me = lax.axis_index("ctx")
    own = (me // 4) * 2 + lax.rem(me, 2)
    for k, out_ref in enumerate((kept_ref,) + sent_refs):
        block = own_ref[own ^ k] + other_ref[own ^ k].astype(jnp.float32)
        out_ref[...] = block.astype(out_ref.dtype)


def sum_kernel(own_ref, *refs):
    *other_refs, out_ref = refs
    result = own_ref[...]
    for other in other_refs:
        result += other[...].astype(jnp.float32)
    requests, tokens, _ = out_ref.shape
    for b in range(requests):
        out_ref[b] = result[b * tokens : (b + 1) * tokens].astype(out_ref.dtype)


def per_device(
    queries,
    key_absorb,
    latent_cache,
    page_order,
    lengths,
    kerple_scale,
    kerple_rate,
    value_up,
    output_weight,
    *,
    ctx,
):
    requests, query_len, heads, query_width = queries.shape
    keys_dev = latent_cache.shape[1]
    half = query_len * heads
    rows = requests * half
    request_rows = LAT_TILES * half
    width = output_weight.shape[1] // ctx
    chunk = 1024

    hint = pl.CostEstimate(flops=20 * 10**9, bytes_accessed=2**20, transcendentals=0)
    long_hint = pl.CostEstimate(flops=100 * 10**9, bytes_accessed=2**20, transcendentals=0)
    in_hbm = lambda value: pltpu.with_memory_space_constraint(value, pltpu.HBM)
    in_vmem = lambda value: pltpu.with_memory_space_constraint(value, pltpu.VMEM)
    line = ctx // 2
    swap = lambda value, bits: lax.ppermute(value, "ctx", [(i, i ^ bits) for i in range(ctx)])
    packed, again = pl.pallas_call(
        query_kernel,
        in_specs=[pl.BlockSpec(memory_space=pl.ANY)] * 2,
        out_shape=[jax.ShapeDtypeStruct((2 * request_rows + half, LANES), jnp.bfloat16)] * 2,
        scratch_shapes=[
            pltpu.VMEM((rows, query_width), jnp.bfloat16),
            pltpu.VMEM(key_absorb.shape, jnp.bfloat16),
            pltpu.SemaphoreType.DMA((5,)),
        ],
        compiler_params=pltpu.CompilerParams(vmem_limit_bytes=8 * 2**20),
        name="latent_query",
    )(in_hbm(queries.reshape(rows, query_width)), in_hbm(key_absorb))
    columns = (ctx, heads, LANES)
    inv_rate, scale, again = pl.pallas_call(
        column_kernel,
        in_specs=[pl.BlockSpec(memory_space=pltpu.VMEM)] * 2
        + [pl.BlockSpec(memory_space=pl.ANY)],
        out_specs=[pl.BlockSpec(memory_space=pltpu.VMEM)] * 2
        + [pl.BlockSpec(memory_space=pl.ANY)],
        out_shape=[jax.ShapeDtypeStruct(columns, jnp.float32)] * 2
        + [jax.ShapeDtypeStruct(again.shape, again.dtype)],
        input_output_aliases={2: 2},
        compiler_params=pltpu.CompilerParams(vmem_limit_bytes=4 * 2**20),
        name="head_columns",
        cost_estimate=long_hint,
    )(in_hbm(kerple_rate.reshape(1, -1)), in_hbm(kerple_scale.reshape(1, -1)), again)
    column = [swap(packed, 2 * k) for k in reversed(range(1, line))]
    beside = [swap(value, 1) for value in column + [again]]
    gathered = [packed] + column[::-1] + beside[::-1]

    cache = in_vmem(jnp.swapaxes(latent_cache, 1, 2))
    all_rows = ctx * half
    message = (request_rows + STAT_ROWS, LANES)
    in_smem = pl.BlockSpec(memory_space=pltpu.SMEM)
    whole = pl.BlockSpec(memory_space=pltpu.VMEM)
    parts = []
    for b in range(requests):
        near, far = pl.pallas_call(
            functools.partial(attention_kernel, ctx=ctx, b=b),
            in_specs=[in_smem, in_smem] + [whole] * (ctx + 3),
            out_shape=[jax.ShapeDtypeStruct((line,) + message, jnp.bfloat16)] * 2,
            scratch_shapes=[
                pltpu.VMEM((all_rows, LAT + ROPE), jnp.bfloat16),
                pltpu.VMEM((all_rows, LAT), jnp.float32),
                pltpu.VMEM((all_rows, LANES), jnp.float32),
            ]
            + [pltpu.VMEM((all_rows, chunk), jnp.float32)] * 2
            + [pltpu.VMEM((all_rows, chunk), jnp.bfloat16)] * 2
            + [pltpu.VMEM((all_rows, LANES), jnp.float32)] * 2,
            compiler_params=pltpu.CompilerParams(vmem_limit_bytes=8 * 2**20),
            cost_estimate=hint,
            name="attention",
        )(in_hbm(page_order), in_hbm(lengths), *gathered, cache, inv_rate, scale)
        merged = pl.pallas_call(
            merge_kernel,
            out_shape=[jax.ShapeDtypeStruct(message, jnp.bfloat16) for _ in range(line)],
            compiler_params=pltpu.CompilerParams(vmem_limit_bytes=4 * 2**20),
            name="merge",
        )(near, swap(far, 1))
        parts.append(merged[0])
        parts += [swap(merged[k], 2 * k) for k in reversed(range(1, line))]

    tokens = requests * query_len
    weight = in_vmem(output_weight)
    small = pltpu.CompilerParams(vmem_limit_bytes=4 * 2**20)
    far, values = pl.pallas_call(
        output_kernel,
        out_shape=[
            jax.ShapeDtypeStruct((line, tokens, width), jnp.bfloat16),
            jax.ShapeDtypeStruct((8, output_weight.shape[0]), jnp.float32),
        ],
        scratch_shapes=[pltpu.VMEM((rows, LAT), jnp.bfloat16)],
        compiler_params=small,
        cost_estimate=hint,
        name="up_and_far_output",
    )(*parts, in_vmem(value_up), weight)
    near = pl.pallas_call(
        near_kernel,
        out_shape=jax.ShapeDtypeStruct((line, tokens, width), jnp.float32),
        compiler_params=small,
        cost_estimate=hint,
        name="near_output",
    )(values, weight)
    block = (tokens, width)
    kept, *sent = pl.pallas_call(
        add_kernel,
        out_shape=[jax.ShapeDtypeStruct(block, jnp.float32)]
        + [jax.ShapeDtypeStruct(block, jnp.bfloat16)] * 3,
        compiler_params=small,
        name="add_columns",
    )(near, swap(far, 2))
    return pl.pallas_call(
        sum_kernel,
        out_shape=jax.ShapeDtypeStruct((requests, query_len, width), jnp.bfloat16),
        compiler_params=small,
        name="sum_output",
    )(kept, *(swap(part, bits) for part, bits in reversed([*zip(sent, (1, 4, 5))])))


def plain_device(
    queries,
    key_absorb,
    latent_cache,
    page_order,
    lengths,
    kerple_scale,
    kerple_rate,
    value_up,
    output_weight,
    *,
    ctx,
):
    requests, query_len, heads, _ = queries.shape
    width = output_weight.shape[1] // ctx
    latent_query = jnp.einsum(
        "bqhn,hnc->bqhc", queries[..., :NOPE], key_absorb, preferred_element_type=jnp.float32
    ).astype(jnp.bfloat16)
    own_query = jnp.concatenate([latent_query, queries[..., NOPE:]], axis=-1)
    full_query = lax.all_gather(own_query, "ctx", axis=2, tiled=True)
    offsets = jnp.arange(PAGE, dtype=jnp.int32)
    key_pos = (page_order[:, :, None] * PAGE + offsets).reshape(requests, -1)
    query_pos = lengths[:, None] - query_len + jnp.arange(query_len, dtype=jnp.int32)
    distance = query_pos[:, :, None] - key_pos[:, None, :]
    visible = (distance >= 0)[:, :, None, :]
    spread = jnp.maximum(distance, 0).astype(jnp.float32)[:, :, None, :]
    log_bias = kerple_scale[:, None] * jnp.log(1.0 + kerple_rate[:, None] * spread)
    scores = jnp.einsum(
        "bqhc,btc->bqht", full_query, latent_cache, preferred_element_type=jnp.float32
    )
    scores = jnp.where(visible, scores * SOFTMAX_SCALE - log_bias, LOWEST)
    row_max = jnp.max(scores, axis=-1)
    weights = jnp.where(visible, jnp.exp(scores - row_max[..., None]), 0.0)
    summed = jnp.einsum(
        "bqht,btc->bqhc",
        weights.astype(jnp.bfloat16),
        latent_cache[..., :LAT],
        preferred_element_type=jnp.float32,
    )
    factor = jnp.exp(row_max - lax.pmax(row_max, "ctx"))
    shared_total = lax.psum_scatter(
        jnp.sum(weights, axis=-1) * factor, "ctx", scatter_dimension=2, tiled=True
    )
    shared_sum = lax.psum_scatter(
        summed * factor[..., None], "ctx", scatter_dimension=2, tiled=True
    )
    attn_latent = (shared_sum / shared_total[..., None]).astype(jnp.bfloat16)
    up_values = jnp.einsum(
        "bqhc,hcv->bqhv", attn_latent, value_up, preferred_element_type=jnp.float32
    ).astype(jnp.bfloat16)
    partial_out = jnp.dot(
        up_values.reshape(requests * query_len, -1),
        output_weight,
        preferred_element_type=jnp.float32,
    )
    summed_out = lax.psum_scatter(partial_out, "ctx", scatter_dimension=1, tiled=True)
    return summed_out.astype(jnp.bfloat16).reshape(requests, query_len, width)


def solution(mesh):
    ctx = mesh.shape["ctx"]
    in_specs = (
        P("rep", None, "ctx", None),
        P("ctx", None, None),
        P("rep", "ctx", None),
        P("rep", "ctx"),
        P("rep"),
        P(),
        P(),
        P("ctx", None, None),
        P("ctx", None),
    )
    out_specs = P("rep", None, "ctx")

    def device_program(*args):
        heads = args[0].shape[2]
        width = args[-1].shape[1] // ctx
        tiled = ctx == 8 and heads % 16 == 0 and width % LANES == 0
        return (per_device if tiled else plain_device)(*args, ctx=ctx)

    return jax.shard_map(
        device_program, mesh=mesh, in_specs=in_specs, out_specs=out_specs, check_vma=False
    )
```

```python
import functools

import jax
import jax.numpy as jnp
from jax import lax
from jax.experimental import pallas as pl
from jax.experimental.pallas import tpu as pltpu
from jax.sharding import PartitionSpec as P

NOPE = 128
ROPE = 64
LAT = 512
PAGE = 128
LANES = 128
LAT_TILES = LAT // LANES
LOG2E = 1.4426950408889634
SOFTMAX_SCALE = (NOPE + ROPE) ** (-0.5)
LOWEST = -1e30
STAT_ROWS = 16


def head_of_row(shape, heads):
    return lax.rem(lax.broadcasted_iota(jnp.int32, shape, 0), heads)


def query_kernel(queries_hbm, absorb_hbm, out_ref, again_ref, queries_ref, absorb_ref, sems):
    rows = queries_ref.shape[0]
    heads = absorb_ref.shape[0]
    half = rows // 2
    pieces = sems.shape[0] - 1
    group = heads // pieces
    copies = [pltpu.make_async_copy(queries_hbm, queries_ref, sems.at[pieces])] + [
        pltpu.make_async_copy(
            absorb_hbm.at[pl.ds(i * group, group)],
            absorb_ref.at[pl.ds(i * group, group)],
            sems.at[i],
        )
        for i in range(pieces)
    ]
    for copy in copies:
        copy.start()
    copies[0].wait()
    nope = queries_ref[:, :NOPE]
    owner = head_of_row((rows, NOPE), heads)
    latent = jnp.zeros((rows, LAT), jnp.float32)
    for i in range(pieces):
        spread = jnp.concatenate(
            [
                jnp.where(owner == h, nope, jnp.zeros_like(nope))
                for h in range(i * group, (i + 1) * group)
            ],
            axis=1,
        )
        copies[i + 1].wait()
        latent += jnp.dot(
            spread,
            absorb_ref[i * group : (i + 1) * group].reshape(group * NOPE, LAT),
            preferred_element_type=jnp.float32,
        )
    latent = latent.astype(jnp.bfloat16)
    rope = queries_ref[:, NOPE:]
    rope = jnp.concatenate([rope[:half], rope[half:]], axis=1)
    for b in range(2):
        for j in range(LAT_TILES):
            start = (b * LAT_TILES + j) * half
            out_ref[start : start + half, :] = latent[
                b * half : (b + 1) * half, j * LANES : (j + 1) * LANES
            ]
    out_ref[2 * LAT_TILES * half :, :] = rope
    again_ref[...] = out_ref[...]


def column_kernel(rate_ref, scale_ref, through_ref, inv_rate_ref, scales_ref, passed_ref):
    del through_ref, passed_ref
    ctx, heads, _ = inv_rate_ref.shape
    line = ctx // 2
    me = lax.axis_index("ctx")
    for source, target in ((1.0 / rate_ref[...], inv_rate_ref), (scale_ref[...], scales_ref)):
        size = source.shape[1]
        same = lax.broadcasted_iota(jnp.int32, (size, size), 0) == lax.broadcasted_iota(
            jnp.int32, (size, size), 1
        )
        column = jnp.sum(jnp.where(same, source, 0.0), axis=1, keepdims=True)
        column = jnp.broadcast_to(column, (size, LANES)).reshape(ctx, heads, LANES)
        for k in range(ctx):
            owner = me ^ (2 * (k % line) + k // line)
            picked = jnp.zeros((heads, LANES), jnp.float32)
            for device in range(ctx):
                picked = jnp.where(owner == device, column[device], picked)
            target[k] = picked


def attention_kernel(pages_ref, lengths_ref, *refs, ctx, b):
    query_refs, refs = refs[:ctx], refs[ctx:]
    cache_ref, inv_rate, scale, near_ref, far_ref, query, acc, total, *buffers = refs
    scores_of, weights_of, factor_of = buffers[:2], buffers[2:4], buffers[4:]
    rows, chunk = scores_of[0].shape
    half = rows // ctx
    heads = half // 2
    line = ctx // 2
    steps = cache_ref.shape[2] // chunk
    chunk_pages = chunk // PAGE
    request_rows = LAT_TILES * half
    start = b * request_rows

    for k, block in enumerate(query_refs):
        own = slice(k * half, (k + 1) * half)
        for j in range(LAT_TILES):
            query[own, j * LANES : (j + 1) * LANES] = block[
                start + j * half : start + (j + 1) * half, :
            ]
        query[own, LAT:] = block[2 * request_rows :, b * ROPE : (b + 1) * ROPE]

    lane = lax.broadcasted_iota(jnp.int32, (heads, LANES), 1)
    first_pos = lengths_ref[b] - 2

    def raw_scores(at):
        return jnp.dot(
            query[...],
            cache_ref[b, :, at * chunk : (at + 1) * chunk],
            preferred_element_type=jnp.float32,
        )

    def add_products(step):
        weights, factor = weights_of[step % 2], factor_of[step % 2]
        new = lax.dot_general(
            weights[...],
            cache_ref[b, :LAT, step * chunk : (step + 1) * chunk],
            (((1,), (1,)), ((), ())),
            preferred_element_type=jnp.float32,
        )
        for j in range(LAT_TILES):
            at = slice(j * LANES, (j + 1) * LANES)
            acc[:, at] = acc[:, at] * factor[...] + new[:, at] if step else new[:, at]

    top = jnp.full((rows, LANES), LOWEST, jnp.float32)
    ahead = raw_scores(0)
    for step in range(steps):
        scores, weights = scores_of[step % 2], weights_of[step % 2]
        tops = [None, None]
        raw = ahead
        if step + 1 < steps:
            ahead = raw_scores(step + 1)
        for page in range(chunk_pages):
            columns = slice(page * PAGE, (page + 1) * PAGE)
            part = raw[:, columns].reshape(ctx, 2, heads, PAGE)
            base = first_pos - pages_ref[b, step * chunk_pages + page] * PAGE
            values = []
            for q in range(2):
                distance = base + q - lane
                spread = jnp.where(distance >= 0, distance.astype(jnp.float32), jnp.inf)
                logs = jnp.log2(spread[None] + inv_rate[...])
                value = part[:, q] * (SOFTMAX_SCALE * LOG2E) - scale[...] * logs
                tops[q] = value if tops[q] is None else jnp.maximum(tops[q], value)
                values.append(value)
            scores[:, columns] = jnp.stack(values, axis=1).reshape(rows, PAGE)
        lane_top = jnp.stack(tops, axis=1).reshape(rows, LANES)
        before = top
        top = jnp.maximum(before, jnp.max(lane_top, axis=1, keepdims=True))
        factor = jnp.exp2(before - top)
        factor_of[step % 2][...] = factor
        if step:
            add_products(step - 1)
        lane_total = total[...] * factor if step else jnp.zeros((rows, LANES), jnp.float32)
        for page in range(chunk // PAGE):
            columns = slice(page * PAGE, (page + 1) * PAGE)
            value = jnp.exp2(scores[:, columns] - top)
            lane_total += value
            weights[:, columns] = value.astype(jnp.bfloat16)
        total[...] = lane_total
    add_products(steps - 1)

    row_total = jnp.sum(total[...], axis=1, keepdims=True)
    row_total = jnp.broadcast_to(row_total, (rows, LANES))
    seen = row_total > 0.0
    safe = jnp.where(seen, row_total, 1.0)
    share = 1.0 / safe
    for j in range(LAT_TILES):
        columns = slice(j * LANES, (j + 1) * LANES)
        part = (acc[:, columns] * share).astype(jnp.bfloat16).reshape(ctx, half, LANES)
        near_ref[:, j * half : (j + 1) * half, :] = part[:line]
        far_ref[:, j * half : (j + 1) * half, :] = part[line:]
    log_total = jnp.where(seen, top + jnp.log2(safe), LOWEST).reshape(ctx, half, LANES)
    across = jnp.sum(jnp.where(diagonal(half), log_total, 0.0), axis=1, keepdims=True)
    packed = three_parts(across).astype(jnp.bfloat16)
    near_ref[:, request_rows:, :] = packed[:line]
    far_ref[:, request_rows:, :] = packed[line:]


def diagonal(half):
    return lax.broadcasted_iota(jnp.int32, (half, LANES), 0) == lax.broadcasted_iota(
        jnp.int32, (half, LANES), 1
    )


def three_parts(value):
    high = value.astype(jnp.bfloat16).astype(jnp.float32)
    middle = (value - high).astype(jnp.bfloat16).astype(jnp.float32)
    low = value - high - middle
    row = lax.broadcasted_iota(jnp.int32, (value.shape[0], STAT_ROWS, LANES), 1)
    return jnp.where(
        row == 0, high, jnp.where(row == 1, middle, jnp.where(row == 2, low, 0.0))
    )


def logs_of(stats):
    return jnp.sum(stats.astype(jnp.float32), axis=1, keepdims=True)


def as_column(across, half):
    return jnp.sum(jnp.where(diagonal(half), across, 0.0), axis=-1, keepdims=True)


def merge_kernel(own_ref, other_ref, *out_refs):
    request_rows = own_ref.shape[1] - STAT_ROWS
    half = request_rows // LAT_TILES
    own_log = logs_of(own_ref[:, request_rows:, :])
    other_log = logs_of(other_ref[:, request_rows:, :])
    high = jnp.maximum(own_log, other_log)
    own_factor = jnp.exp2(own_log - high)
    other_factor = jnp.exp2(other_log - high)
    both = own_factor + other_factor
    stats = three_parts(high + jnp.log2(both)).astype(jnp.bfloat16)
    own_factor = as_column(own_factor / both, half)
    other_factor = as_column(other_factor / both, half)
    for j in range(LAT_TILES):
        at = slice(j * half, (j + 1) * half)
        merged = (
            own_ref[:, at, :].astype(jnp.float32) * own_factor
            + other_ref[:, at, :].astype(jnp.float32) * other_factor
        ).astype(jnp.bfloat16)
        for k, out_ref in enumerate(out_refs):
            out_ref[at, :] = merged[k]
    for k, out_ref in enumerate(out_refs):
        out_ref[request_rows:, :] = stats[k]


def output_kernel(*refs):
    *part_refs, up_ref, weight_ref, out_ref, values, attn = refs
    heads = up_ref.shape[0]
    half = 2 * heads
    rows = 2 * half
    request_rows = LAT_TILES * half
    for b in range(2):
        parts = part_refs[b * len(part_refs) // 2 : (b + 1) * len(part_refs) // 2]
        logs = logs_of(jnp.stack([part[request_rows:, :] for part in parts]))
        factor = jnp.exp2(logs - jnp.max(logs, axis=0, keepdims=True))
        factor = as_column(factor / jnp.sum(factor, axis=0, keepdims=True), half)
        for j in range(LAT_TILES):
            at = slice(j * half, (j + 1) * half)
            attn[b * half : (b + 1) * half, j * LANES : (j + 1) * LANES] = sum(
                part[at, :].astype(jnp.float32) * factor[k] for k, part in enumerate(parts)
            ).astype(jnp.bfloat16)
    latent = attn[...]
    owner = head_of_row(latent.shape, heads)
    up = jnp.zeros((rows, up_ref.shape[2]), jnp.float32)
    for h in range(heads):
        own = jnp.where(owner == h, latent, jnp.zeros_like(latent))
        up += jnp.dot(own, up_ref[h], preferred_element_type=jnp.float32)
    up = up.astype(jnp.bfloat16)
    owner = head_of_row(up.shape, heads)
    spread = jnp.concatenate(
        [jnp.where(owner == h, up, jnp.zeros_like(up)) for h in range(heads)], axis=1
    )
    token = lax.broadcasted_iota(jnp.int32, (8, rows), 0)
    group = lax.broadcasted_iota(jnp.int32, (8, rows), 1) // heads
    pick = jnp.where(token == group, 1.0, 0.0).astype(jnp.bfloat16)
    values[...] = jnp.dot(pick, spread, preferred_element_type=jnp.float32)
    project(values, weight_ref, out_ref, True)


def project(values, weight_ref, out_ref, far):
    blocks, tokens, width = out_ref.shape
    bit = lax.rem(lax.axis_index("ctx") // 2, 2)
    first = (1 - bit if far else bit) * (2 * width)

    @pl.loop(0, blocks // 2)
    def _(k):
        result = jnp.dot(
            values[...].astype(jnp.bfloat16),
            weight_ref[:, pl.ds(pl.multiple_of(first + k * (4 * width), LANES), 2 * width)],
            preferred_element_type=jnp.float32,
        )
        out_ref[2 * k] = result[:tokens, :width].astype(out_ref.dtype)
        out_ref[2 * k + 1] = result[:tokens, width:].astype(out_ref.dtype)


def near_kernel(values, weight_ref, out_ref):
    project(values, weight_ref, out_ref, False)


def add_kernel(own_ref, other_ref, kept_ref, *sent_refs):
    me = lax.axis_index("ctx")
    own = (me // 4) * 2 + lax.rem(me, 2)
    for k, out_ref in enumerate((kept_ref,) + sent_refs):
        block = own_ref[own ^ k] + other_ref[own ^ k].astype(jnp.float32)
        out_ref[...] = block.astype(out_ref.dtype)


def sum_kernel(own_ref, *refs):
    *other_refs, out_ref = refs
    result = own_ref[...]
    for other in other_refs:
        result += other[...].astype(jnp.float32)
    requests, tokens, _ = out_ref.shape
    for b in range(requests):
        out_ref[b] = result[b * tokens : (b + 1) * tokens].astype(out_ref.dtype)


def per_device(
    queries,
    key_absorb,
    latent_cache,
    page_order,
    lengths,
    kerple_scale,
    kerple_rate,
    value_up,
    output_weight,
    *,
    ctx,
):
    requests, query_len, heads, query_width = queries.shape
    keys_dev = latent_cache.shape[1]
    half = query_len * heads
    rows = requests * half
    request_rows = LAT_TILES * half
    width = output_weight.shape[1] // ctx
    chunk = 1024

    hint = pl.CostEstimate(flops=20 * 10**9, bytes_accessed=2**20, transcendentals=0)
    long_hint = pl.CostEstimate(flops=100 * 10**9, bytes_accessed=2**20, transcendentals=0)
    in_hbm = lambda value: pltpu.with_memory_space_constraint(value, pltpu.HBM)
    in_vmem = lambda value: pltpu.with_memory_space_constraint(value, pltpu.VMEM)
    line = ctx // 2
    swap = lambda value, bits: lax.ppermute(value, "ctx", [(i, i ^ bits) for i in range(ctx)])
    packed, again = pl.pallas_call(
        query_kernel,
        in_specs=[pl.BlockSpec(memory_space=pl.ANY)] * 2,
        out_shape=[jax.ShapeDtypeStruct((2 * request_rows + half, LANES), jnp.bfloat16)] * 2,
        scratch_shapes=[
            pltpu.VMEM((rows, query_width), jnp.bfloat16),
            pltpu.VMEM(key_absorb.shape, jnp.bfloat16),
            pltpu.SemaphoreType.DMA((5,)),
        ],
        compiler_params=pltpu.CompilerParams(vmem_limit_bytes=8 * 2**20),
        name="latent_query",
    )(in_hbm(queries.reshape(rows, query_width)), in_hbm(key_absorb))
    columns = (ctx, heads, LANES)
    inv_rate, scale, again = pl.pallas_call(
        column_kernel,
        in_specs=[pl.BlockSpec(memory_space=pltpu.VMEM)] * 2
        + [pl.BlockSpec(memory_space=pl.ANY)],
        out_specs=[pl.BlockSpec(memory_space=pltpu.VMEM)] * 2
        + [pl.BlockSpec(memory_space=pl.ANY)],
        out_shape=[jax.ShapeDtypeStruct(columns, jnp.float32)] * 2
        + [jax.ShapeDtypeStruct(again.shape, again.dtype)],
        input_output_aliases={2: 2},
        compiler_params=pltpu.CompilerParams(vmem_limit_bytes=4 * 2**20),
        name="head_columns",
        cost_estimate=long_hint,
    )(in_hbm(kerple_rate.reshape(1, -1)), in_hbm(kerple_scale.reshape(1, -1)), again)
    column = [packed] + [swap(packed, 2 * k) for k in range(1, line)]
    gathered = column + [swap(value, 1) for value in [again] + column[1:]]

    cache = in_vmem(jnp.swapaxes(latent_cache, 1, 2))
    all_rows = ctx * half
    message = (request_rows + STAT_ROWS, LANES)
    in_smem = pl.BlockSpec(memory_space=pltpu.SMEM)
    whole = pl.BlockSpec(memory_space=pltpu.VMEM)
    parts = []
    for b in range(requests):
        near, far = pl.pallas_call(
            functools.partial(attention_kernel, ctx=ctx, b=b),
            in_specs=[in_smem, in_smem] + [whole] * (ctx + 3),
            out_shape=[jax.ShapeDtypeStruct((line,) + message, jnp.bfloat16)] * 2,
            scratch_shapes=[
                pltpu.VMEM((all_rows, LAT + ROPE), jnp.bfloat16),
                pltpu.VMEM((all_rows, LAT), jnp.float32),
                pltpu.VMEM((all_rows, LANES), jnp.float32),
            ]
            + [pltpu.VMEM((all_rows, chunk), jnp.float32)] * 2
            + [pltpu.VMEM((all_rows, chunk), jnp.bfloat16)] * 2
            + [pltpu.VMEM((all_rows, LANES), jnp.float32)] * 2,
            compiler_params=pltpu.CompilerParams(vmem_limit_bytes=8 * 2**20),
            cost_estimate=hint,
            name="attention",
        )(in_hbm(page_order), in_hbm(lengths), *gathered, cache, inv_rate, scale)
        merged = pl.pallas_call(
            merge_kernel,
            out_shape=[jax.ShapeDtypeStruct(message, jnp.bfloat16) for _ in range(line)],
            compiler_params=pltpu.CompilerParams(vmem_limit_bytes=4 * 2**20),
            name="merge",
        )(near, swap(far, 1))
        parts.append(merged[0])
        parts += [swap(merged[k], 2 * k) for k in reversed(range(1, line))]

    tokens = requests * query_len
    weight = in_vmem(output_weight)
    small = pltpu.CompilerParams(vmem_limit_bytes=4 * 2**20)
    far, values = pl.pallas_call(
        output_kernel,
        out_shape=[
            jax.ShapeDtypeStruct((line, tokens, width), jnp.bfloat16),
            jax.ShapeDtypeStruct((8, output_weight.shape[0]), jnp.float32),
        ],
        scratch_shapes=[pltpu.VMEM((rows, LAT), jnp.bfloat16)],
        compiler_params=small,
        cost_estimate=hint,
        name="up_and_far_output",
    )(*parts, in_vmem(value_up), weight)
    near = pl.pallas_call(
        near_kernel,
        out_shape=jax.ShapeDtypeStruct((line, tokens, width), jnp.float32),
        compiler_params=small,
        cost_estimate=hint,
        name="near_output",
    )(values, weight)
    block = (tokens, width)
    kept, *sent = pl.pallas_call(
        add_kernel,
        out_shape=[jax.ShapeDtypeStruct(block, jnp.float32)]
        + [jax.ShapeDtypeStruct(block, jnp.bfloat16)] * 3,
        compiler_params=small,
        name="add_columns",
    )(near, swap(far, 2))
    return pl.pallas_call(
        sum_kernel,
        out_shape=jax.ShapeDtypeStruct((requests, query_len, width), jnp.bfloat16),
        compiler_params=small,
        name="sum_output",
    )(kept, *(swap(part, bits) for part, bits in reversed([*zip(sent, (1, 4, 5))])))


def plain_device(
    queries,
    key_absorb,
    latent_cache,
    page_order,
    lengths,
    kerple_scale,
    kerple_rate,
    value_up,
    output_weight,
    *,
    ctx,
):
    requests, query_len, heads, _ = queries.shape
    width = output_weight.shape[1] // ctx
    latent_query = jnp.einsum(
        "bqhn,hnc->bqhc", queries[..., :NOPE], key_absorb, preferred_element_type=jnp.float32
    ).astype(jnp.bfloat16)
    own_query = jnp.concatenate([latent_query, queries[..., NOPE:]], axis=-1)
    full_query = lax.all_gather(own_query, "ctx", axis=2, tiled=True)
    offsets = jnp.arange(PAGE, dtype=jnp.int32)
    key_pos = (page_order[:, :, None] * PAGE + offsets).reshape(requests, -1)
    query_pos = lengths[:, None] - query_len + jnp.arange(query_len, dtype=jnp.int32)
    distance = query_pos[:, :, None] - key_pos[:, None, :]
    visible = (distance >= 0)[:, :, None, :]
    spread = jnp.maximum(distance, 0).astype(jnp.float32)[:, :, None, :]
    log_bias = kerple_scale[:, None] * jnp.log(1.0 + kerple_rate[:, None] * spread)
    scores = jnp.einsum(
        "bqhc,btc->bqht", full_query, latent_cache, preferred_element_type=jnp.float32
    )
    scores = jnp.where(visible, scores * SOFTMAX_SCALE - log_bias, LOWEST)
    row_max = jnp.max(scores, axis=-1)
    weights = jnp.where(visible, jnp.exp(scores - row_max[..., None]), 0.0)
    summed = jnp.einsum(
        "bqht,btc->bqhc",
        weights.astype(jnp.bfloat16),
        latent_cache[..., :LAT],
        preferred_element_type=jnp.float32,
    )
    factor = jnp.exp(row_max - lax.pmax(row_max, "ctx"))
    shared_total = lax.psum_scatter(
        jnp.sum(weights, axis=-1) * factor, "ctx", scatter_dimension=2, tiled=True
    )
    shared_sum = lax.psum_scatter(
        summed * factor[..., None], "ctx", scatter_dimension=2, tiled=True
    )
    attn_latent = (shared_sum / shared_total[..., None]).astype(jnp.bfloat16)
    up_values = jnp.einsum(
        "bqhc,hcv->bqhv", attn_latent, value_up, preferred_element_type=jnp.float32
    ).astype(jnp.bfloat16)
    partial_out = jnp.dot(
        up_values.reshape(requests * query_len, -1),
        output_weight,
        preferred_element_type=jnp.float32,
    )
    summed_out = lax.psum_scatter(partial_out, "ctx", scatter_dimension=1, tiled=True)
    return summed_out.astype(jnp.bfloat16).reshape(requests, query_len, width)


def solution(mesh):
    ctx = mesh.shape["ctx"]
    in_specs = (
        P("rep", None, "ctx", None),
        P("ctx", None, None),
        P("rep", "ctx", None),
        P("rep", "ctx"),
        P("rep"),
        P(),
        P(),
        P("ctx", None, None),
        P("ctx", None),
    )
    out_specs = P("rep", None, "ctx")

    def device_program(*args):
        heads = args[0].shape[2]
        width = args[-1].shape[1] // ctx
        tiled = ctx == 8 and heads % 16 == 0 and width % LANES == 0
        return (per_device if tiled else plain_device)(*args, ctx=ctx)

    return jax.shard_map(
        device_program, mesh=mesh, in_specs=in_specs, out_specs=out_specs, check_vma=False
    )
```

```python
import functools

import jax
import jax.numpy as jnp
from jax import lax
from jax.experimental import pallas as pl
from jax.experimental.pallas import tpu as pltpu
from jax.sharding import PartitionSpec as P

NOPE = 128
ROPE = 64
LAT = 512
PAGE = 128
LANES = 128
LAT_TILES = LAT // LANES
LOG2E = 1.4426950408889634
SOFTMAX_SCALE = (NOPE + ROPE) ** (-0.5)
LOWEST = -1e30
STAT_ROWS = 16


def head_of_row(shape, heads):
    return lax.rem(lax.broadcasted_iota(jnp.int32, shape, 0), heads)


def query_kernel(queries_hbm, absorb_hbm, out_ref, again_ref, queries_ref, absorb_ref, sems):
    rows = queries_ref.shape[0]
    heads = absorb_ref.shape[0]
    half = rows // 2
    pieces = sems.shape[0] - 1
    group = heads // pieces
    copies = [pltpu.make_async_copy(queries_hbm, queries_ref, sems.at[pieces])] + [
        pltpu.make_async_copy(
            absorb_hbm.at[pl.ds(i * group, group)],
            absorb_ref.at[pl.ds(i * group, group)],
            sems.at[i],
        )
        for i in range(pieces)
    ]
    for copy in copies:
        copy.start()
    copies[0].wait()
    nope = queries_ref[:, :NOPE]
    owner = head_of_row((rows, NOPE), heads)
    latent = jnp.zeros((rows, LAT), jnp.float32)
    for i in range(pieces):
        spread = jnp.concatenate(
            [
                jnp.where(owner == h, nope, jnp.zeros_like(nope))
                for h in range(i * group, (i + 1) * group)
            ],
            axis=1,
        )
        copies[i + 1].wait()
        latent += jnp.dot(
            spread,
            absorb_ref[i * group : (i + 1) * group].reshape(group * NOPE, LAT),
            preferred_element_type=jnp.float32,
        )
    latent = latent.astype(jnp.bfloat16)
    rope = queries_ref[:, NOPE:]
    rope = jnp.concatenate([rope[:half], rope[half:]], axis=1)
    for b in range(2):
        for j in range(LAT_TILES):
            start = (b * LAT_TILES + j) * half
            out_ref[start : start + half, :] = latent[
                b * half : (b + 1) * half, j * LANES : (j + 1) * LANES
            ]
    out_ref[2 * LAT_TILES * half :, :] = rope
    again_ref[...] = out_ref[...]


def column_kernel(rate_ref, scale_ref, through_ref, inv_rate_ref, scales_ref, passed_ref):
    del through_ref, passed_ref
    ctx, heads, _ = inv_rate_ref.shape
    line = ctx // 2
    me = lax.axis_index("ctx")
    for source, target in ((1.0 / rate_ref[...], inv_rate_ref), (scale_ref[...], scales_ref)):
        size = source.shape[1]
        same = lax.broadcasted_iota(jnp.int32, (size, size), 0) == lax.broadcasted_iota(
            jnp.int32, (size, size), 1
        )
        column = jnp.sum(jnp.where(same, source, 0.0), axis=1, keepdims=True)
        column = jnp.broadcast_to(column, (size, LANES)).reshape(ctx, heads, LANES)
        for k in range(ctx):
            owner = me ^ (2 * (k % line) + k // line)
            picked = jnp.zeros((heads, LANES), jnp.float32)
            for device in range(ctx):
                picked = jnp.where(owner == device, column[device], picked)
            target[k] = picked


def attention_kernel(pages_ref, lengths_ref, *refs, ctx, b):
    query_refs, refs = refs[:ctx], refs[ctx:]
    cache_ref, inv_rate, scale, near_ref, far_ref, query, acc, total, *buffers = refs
    scores_of, weights_of, factor_of = buffers[:2], buffers[2:4], buffers[4:]
    rows, chunk = scores_of[0].shape
    half = rows // ctx
    heads = half // 2
    line = ctx // 2
    steps = cache_ref.shape[2] // chunk
    pair_width = 2 * PAGE
    pairs = chunk // pair_width
    request_rows = LAT_TILES * half
    start = b * request_rows

    for k, block in enumerate(query_refs):
        own = slice(k * half, (k + 1) * half)
        for j in range(LAT_TILES):
            query[own, j * LANES : (j + 1) * LANES] = block[
                start + j * half : start + (j + 1) * half, :
            ]
        query[own, LAT:] = block[2 * request_rows :, b * ROPE : (b + 1) * ROPE]

    lane = lax.broadcasted_iota(jnp.int32, (heads, LANES), 1)
    first_pos = lengths_ref[b] - 2

    def raw_scores(at):
        return jnp.dot(
            query[...],
            cache_ref[b, :, at * pair_width : (at + 1) * pair_width],
            preferred_element_type=jnp.float32,
        )

    def add_products(step):
        weights, factor = weights_of[step % 2], factor_of[step % 2]
        for columns in (slice(0, LAT // 2), slice(LAT // 2, LAT)):
            new = lax.dot_general(
                weights[...],
                cache_ref[b, columns, step * chunk : (step + 1) * chunk],
                (((1,), (1,)), ((), ())),
                preferred_element_type=jnp.float32,
            )
            for j in range(columns.start, columns.stop, LANES):
                part = new[:, j - columns.start : j - columns.start + LANES]
                at = slice(j, j + LANES)
                acc[:, at] = acc[:, at] * factor[...] + part if step else part

    top = jnp.full((rows, LANES), LOWEST, jnp.float32)
    ahead = raw_scores(0)
    for step in range(steps):
        scores, weights = scores_of[step % 2], weights_of[step % 2]
        tops = [None, None]
        for pair in range(pairs):
            raw = ahead
            at = step * pairs + pair
            if at + 1 < steps * pairs:
                ahead = raw_scores(at + 1)
            for side in range(2):
                page = pair * 2 + side
                columns = slice(page * PAGE, (page + 1) * PAGE)
                part = raw[:, side * PAGE : (side + 1) * PAGE].reshape(ctx, 2, heads, PAGE)
                base = first_pos - pages_ref[b, step * (chunk // PAGE) + page] * PAGE
                values = []
                for q in range(2):
                    distance = base + q - lane
                    spread = jnp.where(distance >= 0, distance.astype(jnp.float32), jnp.inf)
                    logs = jnp.log2(spread[None] + inv_rate[...])
                    value = part[:, q] * (SOFTMAX_SCALE * LOG2E) - scale[...] * logs
                    tops[q] = value if tops[q] is None else jnp.maximum(tops[q], value)
                    values.append(value)
                scores[:, columns] = jnp.stack(values, axis=1).reshape(rows, PAGE)
        lane_top = jnp.stack(tops, axis=1).reshape(rows, LANES)
        before = top
        top = jnp.maximum(before, jnp.max(lane_top, axis=1, keepdims=True))
        factor = jnp.exp2(before - top)
        factor_of[step % 2][...] = factor
        if step:
            add_products(step - 1)
        lane_total = total[...] * factor if step else jnp.zeros((rows, LANES), jnp.float32)
        for page in range(chunk // PAGE):
            columns = slice(page * PAGE, (page + 1) * PAGE)
            value = jnp.exp2(scores[:, columns] - top)
            lane_total += value
            weights[:, columns] = value.astype(jnp.bfloat16)
        total[...] = lane_total
    add_products(steps - 1)

    row_total = jnp.sum(total[...], axis=1, keepdims=True)
    row_total = jnp.broadcast_to(row_total, (rows, LANES))
    seen = row_total > 0.0
    safe = jnp.where(seen, row_total, 1.0)
    share = 1.0 / safe
    for j in range(LAT_TILES):
        columns = slice(j * LANES, (j + 1) * LANES)
        part = (acc[:, columns] * share).astype(jnp.bfloat16).reshape(ctx, half, LANES)
        near_ref[:, j * half : (j + 1) * half, :] = part[:line]
        far_ref[:, j * half : (j + 1) * half, :] = part[line:]
    log_total = jnp.where(seen, top + jnp.log2(safe), LOWEST).reshape(ctx, half, LANES)
    across = jnp.sum(jnp.where(diagonal(half), log_total, 0.0), axis=1, keepdims=True)
    packed = three_parts(across).astype(jnp.bfloat16)
    near_ref[:, request_rows:, :] = packed[:line]
    far_ref[:, request_rows:, :] = packed[line:]


def diagonal(half):
    return lax.broadcasted_iota(jnp.int32, (half, LANES), 0) == lax.broadcasted_iota(
        jnp.int32, (half, LANES), 1
    )


def three_parts(value):
    high = value.astype(jnp.bfloat16).astype(jnp.float32)
    middle = (value - high).astype(jnp.bfloat16).astype(jnp.float32)
    low = value - high - middle
    row = lax.broadcasted_iota(jnp.int32, (value.shape[0], STAT_ROWS, LANES), 1)
    return jnp.where(
        row == 0, high, jnp.where(row == 1, middle, jnp.where(row == 2, low, 0.0))
    )


def logs_of(stats):
    return jnp.sum(stats.astype(jnp.float32), axis=1, keepdims=True)


def as_column(across, half):
    return jnp.sum(jnp.where(diagonal(half), across, 0.0), axis=-1, keepdims=True)


def merge_kernel(own_ref, other_ref, *out_refs):
    request_rows = own_ref.shape[1] - STAT_ROWS
    half = request_rows // LAT_TILES
    own_log = logs_of(own_ref[:, request_rows:, :])
    other_log = logs_of(other_ref[:, request_rows:, :])
    high = jnp.maximum(own_log, other_log)
    own_factor = jnp.exp2(own_log - high)
    other_factor = jnp.exp2(other_log - high)
    both = own_factor + other_factor
    stats = three_parts(high + jnp.log2(both)).astype(jnp.bfloat16)
    own_factor = as_column(own_factor / both, half)
    other_factor = as_column(other_factor / both, half)
    for j in range(LAT_TILES):
        at = slice(j * half, (j + 1) * half)
        merged = (
            own_ref[:, at, :].astype(jnp.float32) * own_factor
            + other_ref[:, at, :].astype(jnp.float32) * other_factor
        ).astype(jnp.bfloat16)
        for k, out_ref in enumerate(out_refs):
            out_ref[at, :] = merged[k]
    for k, out_ref in enumerate(out_refs):
        out_ref[request_rows:, :] = stats[k]


def output_kernel(*refs):
    *part_refs, up_ref, weight_ref, out_ref, values, attn = refs
    heads = up_ref.shape[0]
    half = 2 * heads
    rows = 2 * half
    request_rows = LAT_TILES * half
    for b in range(2):
        parts = part_refs[b * len(part_refs) // 2 : (b + 1) * len(part_refs) // 2]
        logs = logs_of(jnp.stack([part[request_rows:, :] for part in parts]))
        factor = jnp.exp2(logs - jnp.max(logs, axis=0, keepdims=True))
        factor = as_column(factor / jnp.sum(factor, axis=0, keepdims=True), half)
        for j in range(LAT_TILES):
            at = slice(j * half, (j + 1) * half)
            attn[b * half : (b + 1) * half, j * LANES : (j + 1) * LANES] = sum(
                part[at, :].astype(jnp.float32) * factor[k] for k, part in enumerate(parts)
            ).astype(jnp.bfloat16)
    latent = attn[...]
    owner = head_of_row(latent.shape, heads)
    up = jnp.zeros((rows, up_ref.shape[2]), jnp.float32)
    for h in range(heads):
        own = jnp.where(owner == h, latent, jnp.zeros_like(latent))
        up += jnp.dot(own, up_ref[h], preferred_element_type=jnp.float32)
    up = up.astype(jnp.bfloat16)
    owner = head_of_row(up.shape, heads)
    spread = jnp.concatenate(
        [jnp.where(owner == h, up, jnp.zeros_like(up)) for h in range(heads)], axis=1
    )
    token = lax.broadcasted_iota(jnp.int32, (8, rows), 0)
    group = lax.broadcasted_iota(jnp.int32, (8, rows), 1) // heads
    pick = jnp.where(token == group, 1.0, 0.0).astype(jnp.bfloat16)
    values[...] = jnp.dot(pick, spread, preferred_element_type=jnp.float32)
    project(values, weight_ref, out_ref, True)


def project(values, weight_ref, out_ref, far):
    blocks, tokens, width = out_ref.shape
    bit = lax.rem(lax.axis_index("ctx") // 2, 2)
    first = (1 - bit if far else bit) * (2 * width)

    @pl.loop(0, blocks // 2)
    def _(k):
        result = jnp.dot(
            values[...].astype(jnp.bfloat16),
            weight_ref[:, pl.ds(pl.multiple_of(first + k * (4 * width), LANES), 2 * width)],
            preferred_element_type=jnp.float32,
        )
        out_ref[2 * k] = result[:tokens, :width].astype(out_ref.dtype)
        out_ref[2 * k + 1] = result[:tokens, width:].astype(out_ref.dtype)


def near_kernel(values, weight_ref, out_ref):
    project(values, weight_ref, out_ref, False)


def add_kernel(own_ref, other_ref, kept_ref, *sent_refs):
    me = lax.axis_index("ctx")
    own = (me // 4) * 2 + lax.rem(me, 2)
    for k, out_ref in enumerate((kept_ref,) + sent_refs):
        block = own_ref[own ^ k] + other_ref[own ^ k].astype(jnp.float32)
        out_ref[...] = block.astype(out_ref.dtype)


def sum_kernel(own_ref, *refs):
    *other_refs, out_ref = refs
    result = own_ref[...]
    for other in other_refs:
        result += other[...].astype(jnp.float32)
    requests, tokens, _ = out_ref.shape
    for b in range(requests):
        out_ref[b] = result[b * tokens : (b + 1) * tokens].astype(out_ref.dtype)


def per_device(
    queries,
    key_absorb,
    latent_cache,
    page_order,
    lengths,
    kerple_scale,
    kerple_rate,
    value_up,
    output_weight,
    *,
    ctx,
):
    requests, query_len, heads, query_width = queries.shape
    keys_dev = latent_cache.shape[1]
    half = query_len * heads
    rows = requests * half
    request_rows = LAT_TILES * half
    width = output_weight.shape[1] // ctx
    chunk = 1024

    hint = pl.CostEstimate(flops=20 * 10**9, bytes_accessed=2**20, transcendentals=0)
    long_hint = pl.CostEstimate(flops=100 * 10**9, bytes_accessed=2**20, transcendentals=0)
    in_hbm = lambda value: pltpu.with_memory_space_constraint(value, pltpu.HBM)
    in_vmem = lambda value: pltpu.with_memory_space_constraint(value, pltpu.VMEM)
    line = ctx // 2
    swap = lambda value, bits: lax.ppermute(value, "ctx", [(i, i ^ bits) for i in range(ctx)])
    packed, again = pl.pallas_call(
        query_kernel,
        in_specs=[pl.BlockSpec(memory_space=pl.ANY)] * 2,
        out_shape=[jax.ShapeDtypeStruct((2 * request_rows + half, LANES), jnp.bfloat16)] * 2,
        scratch_shapes=[
            pltpu.VMEM((rows, query_width), jnp.bfloat16),
            pltpu.VMEM(key_absorb.shape, jnp.bfloat16),
            pltpu.SemaphoreType.DMA((5,)),
        ],
        compiler_params=pltpu.CompilerParams(vmem_limit_bytes=8 * 2**20),
        name="latent_query",
    )(in_hbm(queries.reshape(rows, query_width)), in_hbm(key_absorb))
    columns = (ctx, heads, LANES)
    inv_rate, scale, again = pl.pallas_call(
        column_kernel,
        in_specs=[pl.BlockSpec(memory_space=pltpu.VMEM)] * 2
        + [pl.BlockSpec(memory_space=pl.ANY)],
        out_specs=[pl.BlockSpec(memory_space=pltpu.VMEM)] * 2
        + [pl.BlockSpec(memory_space=pl.ANY)],
        out_shape=[jax.ShapeDtypeStruct(columns, jnp.float32)] * 2
        + [jax.ShapeDtypeStruct(again.shape, again.dtype)],
        input_output_aliases={2: 2},
        compiler_params=pltpu.CompilerParams(vmem_limit_bytes=4 * 2**20),
        name="head_columns",
        cost_estimate=long_hint,
    )(in_hbm(kerple_rate.reshape(1, -1)), in_hbm(kerple_scale.reshape(1, -1)), again)
    column = [packed] + [swap(packed, 2 * k) for k in range(1, line)]
    gathered = column + [swap(value, 1) for value in [again] + column[1:]]

    cache = in_vmem(jnp.swapaxes(latent_cache, 1, 2))
    all_rows = ctx * half
    message = (request_rows + STAT_ROWS, LANES)
    in_smem = pl.BlockSpec(memory_space=pltpu.SMEM)
    whole = pl.BlockSpec(memory_space=pltpu.VMEM)
    parts = []
    for b in range(requests):
        near, far = pl.pallas_call(
            functools.partial(attention_kernel, ctx=ctx, b=b),
            in_specs=[in_smem, in_smem] + [whole] * (ctx + 3),
            out_shape=[jax.ShapeDtypeStruct((line,) + message, jnp.bfloat16)] * 2,
            scratch_shapes=[
                pltpu.VMEM((all_rows, LAT + ROPE), jnp.bfloat16),
                pltpu.VMEM((all_rows, LAT), jnp.float32),
                pltpu.VMEM((all_rows, LANES), jnp.float32),
            ]
            + [pltpu.VMEM((all_rows, chunk), jnp.float32)] * 2
            + [pltpu.VMEM((all_rows, chunk), jnp.bfloat16)] * 2
            + [pltpu.VMEM((all_rows, LANES), jnp.float32)] * 2,
            compiler_params=pltpu.CompilerParams(vmem_limit_bytes=8 * 2**20),
            cost_estimate=hint,
            name="attention",
        )(in_hbm(page_order), in_hbm(lengths), *gathered, cache, inv_rate, scale)
        merged = pl.pallas_call(
            merge_kernel,
            out_shape=[jax.ShapeDtypeStruct(message, jnp.bfloat16) for _ in range(line)],
            compiler_params=pltpu.CompilerParams(vmem_limit_bytes=4 * 2**20),
            name="merge",
        )(near, swap(far, 1))
        parts.append(merged[0])
        parts += [swap(merged[k], 2 * k) for k in (line // 2, *range(line // 2 + 1, line), *range(1, line // 2))]

    tokens = requests * query_len
    weight = in_vmem(output_weight)
    small = pltpu.CompilerParams(vmem_limit_bytes=4 * 2**20)
    far, values = pl.pallas_call(
        output_kernel,
        out_shape=[
            jax.ShapeDtypeStruct((line, tokens, width), jnp.bfloat16),
            jax.ShapeDtypeStruct((8, output_weight.shape[0]), jnp.float32),
        ],
        scratch_shapes=[pltpu.VMEM((rows, LAT), jnp.bfloat16)],
        compiler_params=small,
        cost_estimate=hint,
        name="up_and_far_output",
    )(*parts, in_vmem(value_up), weight)
    near = pl.pallas_call(
        near_kernel,
        out_shape=jax.ShapeDtypeStruct((line, tokens, width), jnp.float32),
        compiler_params=small,
        cost_estimate=hint,
        name="near_output",
    )(values, weight)
    block = (tokens, width)
    kept, *sent = pl.pallas_call(
        add_kernel,
        out_shape=[jax.ShapeDtypeStruct(block, jnp.float32)]
        + [jax.ShapeDtypeStruct(block, jnp.bfloat16)] * 3,
        compiler_params=small,
        name="add_columns",
    )(near, swap(far, 2))
    return pl.pallas_call(
        sum_kernel,
        out_shape=jax.ShapeDtypeStruct((requests, query_len, width), jnp.bfloat16),
        compiler_params=small,
        name="sum_output",
    )(kept, *(swap(part, bits) for part, bits in reversed([*zip(sent, (1, 4, 5))])))


def plain_device(
    queries,
    key_absorb,
    latent_cache,
    page_order,
    lengths,
    kerple_scale,
    kerple_rate,
    value_up,
    output_weight,
    *,
    ctx,
):
    requests, query_len, heads, _ = queries.shape
    width = output_weight.shape[1] // ctx
    latent_query = jnp.einsum(
        "bqhn,hnc->bqhc", queries[..., :NOPE], key_absorb, preferred_element_type=jnp.float32
    ).astype(jnp.bfloat16)
    own_query = jnp.concatenate([latent_query, queries[..., NOPE:]], axis=-1)
    full_query = lax.all_gather(own_query, "ctx", axis=2, tiled=True)
    offsets = jnp.arange(PAGE, dtype=jnp.int32)
    key_pos = (page_order[:, :, None] * PAGE + offsets).reshape(requests, -1)
    query_pos = lengths[:, None] - query_len + jnp.arange(query_len, dtype=jnp.int32)
    distance = query_pos[:, :, None] - key_pos[:, None, :]
    visible = (distance >= 0)[:, :, None, :]
    spread = jnp.maximum(distance, 0).astype(jnp.float32)[:, :, None, :]
    log_bias = kerple_scale[:, None] * jnp.log(1.0 + kerple_rate[:, None] * spread)
    scores = jnp.einsum(
        "bqhc,btc->bqht", full_query, latent_cache, preferred_element_type=jnp.float32
    )
    scores = jnp.where(visible, scores * SOFTMAX_SCALE - log_bias, LOWEST)
    row_max = jnp.max(scores, axis=-1)
    weights = jnp.where(visible, jnp.exp(scores - row_max[..., None]), 0.0)
    summed = jnp.einsum(
        "bqht,btc->bqhc",
        weights.astype(jnp.bfloat16),
        latent_cache[..., :LAT],
        preferred_element_type=jnp.float32,
    )
    factor = jnp.exp(row_max - lax.pmax(row_max, "ctx"))
    shared_total = lax.psum_scatter(
        jnp.sum(weights, axis=-1) * factor, "ctx", scatter_dimension=2, tiled=True
    )
    shared_sum = lax.psum_scatter(
        summed * factor[..., None], "ctx", scatter_dimension=2, tiled=True
    )
    attn_latent = (shared_sum / shared_total[..., None]).astype(jnp.bfloat16)
    up_values = jnp.einsum(
        "bqhc,hcv->bqhv", attn_latent, value_up, preferred_element_type=jnp.float32
    ).astype(jnp.bfloat16)
    partial_out = jnp.dot(
        up_values.reshape(requests * query_len, -1),
        output_weight,
        preferred_element_type=jnp.float32,
    )
    summed_out = lax.psum_scatter(partial_out, "ctx", scatter_dimension=1, tiled=True)
    return summed_out.astype(jnp.bfloat16).reshape(requests, query_len, width)


def solution(mesh):
    ctx = mesh.shape["ctx"]
    in_specs = (
        P("rep", None, "ctx", None),
        P("ctx", None, None),
        P("rep", "ctx", None),
        P("rep", "ctx"),
        P("rep"),
        P(),
        P(),
        P("ctx", None, None),
        P("ctx", None),
    )
    out_specs = P("rep", None, "ctx")

    def device_program(*args):
        heads = args[0].shape[2]
        width = args[-1].shape[1] // ctx
        tiled = ctx == 8 and heads % 16 == 0 and width % LANES == 0
        return (per_device if tiled else plain_device)(*args, ctx=ctx)

    return jax.shard_map(
        device_program, mesh=mesh, in_specs=in_specs, out_specs=out_specs, check_vma=False
    )
```
